128 devices in a mesh: section: 2 (over core), block: 64 (over x, z, y).
Axes of the slice: x: 4, y: 4, z: 4, core: 2. Of those that a mesh axis runs over, the one named last changes fastest.
Arguments:
- state: float32 [2, 64, 5, 32, 1024], P('section', 'block'), may hold values from -1 to 3.5, as said below
- mean_flow: float32 [64, 5, 32, 1024], P('block'), may hold values from -0.5 to 1.5, as said below
- les_owner: int32 [64], replicated, may hold values from 0 to 63, each once
- ac_owner: int32 [64], replicated, may hold values from 0 to 63, each once
- les_nbr: int32 [64, 6], replicated, may hold values from -1 to 63, as said below
- ac_nbr: int32 [64, 6], replicated, may hold values from -1 to 63, as said below
- coupling: int32 [64], replicated, may hold values from 0 to 63, each once
Outputs:
- advanced: float32 [2, 64, 5, 32, 1024], P('section', 'block')
The draws below stay inside these ranges and needn't reach their ends.
Inputs may be any that keep to these rules, and one draw needn't show every extreme that they name: `state`: section 0: density 1 to 1.5, momenta -0.4 to 0.4, pressure 0.4 (E - m.m / (2 r)) 0.7 to 1.3. Section 1: all entries -1 to 1. `mean_flow`: mean density 0.8 to 1.5, mean velocities -0.5 to 0.5, mean pressure 0.7 to 1.3. `les_nbr`: blocks sit on a 4 x 4 x 64/16 grid of equal blocks; an entry names the block beside it across that face, and that block names it back across the opposite face. `ac_nbr`: blocks sit on a 4 x 4 x 64/16 grid of equal blocks; an entry names the block beside it across that face, and that block names it back across the opposite face.
All inputs are finite; a program needn't handle non-finite values.
Results may differ from the reference program's by a relative error of at most 0.0003.
Values may be sent and summed in bfloat16 or wider, within the bound.
A program may use at most 128 MiB of HBM per device.

```python
import jax
import jax.numpy as jnp
from jax import lax

BS = 32
STEPS = 2
NBLK = 64


def grid_neighbours(key):
    layers_z = NBLK // 16
    position = jax.random.permutation(key, NBLK).astype(jnp.int32)
    coord_x = position // (4 * layers_z)
    coord_y = position // layers_z % 4
    coord_z = position % layers_z
    block_at = jnp.argsort(position).astype(jnp.int32)
    offsets = [(-1, 0, 0), (1, 0, 0), (0, -1, 0), (0, 1, 0), (0, 0, -1), (0, 0, 1)]
    columns = []
    for step_x, step_y, step_z in offsets:
        next_x = coord_x + step_x
        next_y = coord_y + step_y
        next_z = coord_z + step_z
        inside = (next_x >= 0) & (next_x < 4) & (next_y >= 0) & (next_y < 4) & (next_z >= 0) & (next_z < layers_z)
        target = jnp.clip(next_x * 4 * layers_z + next_y * layers_z + next_z, 0, NBLK - 1)
        columns.append(jnp.where(inside, block_at[target], -1))
    return jnp.stack(columns, axis=1).astype(jnp.int32)


def draw_les_nbr(key, part):
    return grid_neighbours(jax.random.fold_in(key, 11))


def draw_ac_nbr(key, part):
    return grid_neighbours(jax.random.fold_in(key, 23))


def draw_state(key, part):
    keys = jax.random.split(jax.random.fold_in(key, 37), 2)
    shape_one = (NBLK, BS, BS * BS)
    uniform_part = jax.random.uniform(keys[0], (5,) + shape_one, jnp.float32)
    density = 1.0 + 0.5 * uniform_part[0]
    momentum = -0.4 + 0.8 * uniform_part[1:4]
    pressure = 0.7 + 0.6 * uniform_part[4]
    energy = pressure / 0.4 + 0.5 * jnp.sum(momentum * momentum, axis=0) / density
    les_part = jnp.concatenate([density[None], momentum, energy[None]], axis=0)
    acoustic = jax.random.uniform(keys[1], (5,) + shape_one, jnp.float32, -1.0, 1.0)
    stacked = jnp.stack([les_part, acoustic])
    return jnp.transpose(stacked, (0, 2, 1, 3, 4)).astype(jnp.float32)


def draw_mean_flow(key, part):
    uniform_part = jax.random.uniform(jax.random.fold_in(key, 41), (5, NBLK, BS, BS * BS), jnp.float32)
    density = 0.8 + 0.7 * uniform_part[0]
    velocity = -0.5 + uniform_part[1:4]
    pressure = 0.7 + 0.6 * uniform_part[4]
    stacked = jnp.concatenate([density[None], velocity, pressure[None]], axis=0)
    return jnp.transpose(stacked, (1, 0, 2, 3)).astype(jnp.float32)


def setup_inputs(seed: int = 0) -> dict:
    seeds = jax.random.split(jax.random.key(seed), 8)
    state = draw_state(jax.random.fold_in(seeds[7], 71), 0)
    mean_flow = draw_mean_flow(jax.random.fold_in(seeds[7], 71), 0)
    les_owner = jax.random.permutation(seeds[2], NBLK).astype(jnp.int32)
    ac_owner = jax.random.permutation(seeds[3], NBLK).astype(jnp.int32)
    les_nbr = draw_les_nbr(jax.random.fold_in(seeds[7], 71), 0)
    ac_nbr = draw_ac_nbr(jax.random.fold_in(seeds[7], 71), 0)
    coupling = jax.random.permutation(seeds[6], NBLK).astype(jnp.int32)
    return {"state": state, "mean_flow": mean_flow, "les_owner": les_owner, "ac_owner": ac_owner, "les_nbr": les_nbr, "ac_nbr": ac_nbr, "coupling": coupling}


GAMMA_LESS = 0.4
DT_LES = 0.2
DT_AC = 0.3
VISCOSITY = 0.05
FEEDBACK_GAIN = 0.5


def face_layers(volume):
    num_blocks, num_vars, cube_side, face_cells = volume.shape
    members = [
        volume[:, :, 0, :],
        volume[:, :, cube_side - 1, :],
        volume[:, :, :, 0:cube_side].reshape(num_blocks, num_vars, face_cells),
        volume[:, :, :, (cube_side - 1) * cube_side:].reshape(num_blocks, num_vars, face_cells),
        volume[:, :, :, 0::cube_side].reshape(num_blocks, num_vars, face_cells),
        volume[:, :, :, cube_side - 1::cube_side].reshape(num_blocks, num_vars, face_cells),
    ]
    return jnp.stack(members, axis=1)


def neighbours(volume, halo_cells):
    num_blocks, num_vars, cube_side, face_cells = volume.shape

    def face_grid(direction):
        return halo_cells[:, direction].reshape(num_blocks, num_vars, cube_side, cube_side)

    low_x = jnp.concatenate([halo_cells[:, 0][:, :, None, :], volume[:, :, :-1, :]], axis=2)
    high_x = jnp.concatenate([volume[:, :, 1:, :], halo_cells[:, 1][:, :, None, :]], axis=2)
    low_y = jnp.concatenate([face_grid(2), volume[:, :, :, :-cube_side]], axis=3)
    high_y = jnp.concatenate([volume[:, :, :, cube_side:], face_grid(3)], axis=3)
    z_index = lax.broadcasted_iota(jnp.int32, (1, 1, 1, face_cells), 3) % cube_side
    low_z = jnp.where(z_index == 0, jnp.repeat(face_grid(4), cube_side, axis=3), jnp.roll(volume, 1, axis=3))
    high_z = jnp.where(z_index == cube_side - 1, jnp.repeat(face_grid(5), cube_side, axis=3), jnp.roll(volume, -1, axis=3))
    return ((low_x, high_x), (low_y, high_y), (low_z, high_z))


def primitives(conserved):
    density = conserved[:, 0]
    momentum = conserved[:, 1:4]
    energy = conserved[:, 4]
    velocity = momentum / density[:, None]
    pressure = GAMMA_LESS * (energy - 0.5 * jnp.sum(momentum * velocity, axis=1))
    return momentum, energy, velocity, pressure


def flux_along(conserved, axis_k):
    momentum, energy, velocity, pressure = primitives(conserved)
    normal_speed = velocity[:, axis_k]
    members = [momentum[:, axis_k]]
    for component in range(3):
        entry_term = momentum[:, component] * normal_speed
        if component == axis_k:
            entry_term = entry_term + pressure
        members.append(entry_term)
    members.append((energy + pressure) * normal_speed)
    return jnp.stack(members, axis=1), velocity


def les_both(conserved, halo_cells):
    pairs = neighbours(conserved, halo_cells)
    momentum, energy, velocity, pressure = primitives(conserved)
    flux_sum = jnp.zeros_like(conserved)
    laplace = -6.0 * conserved
    gradient = []
    for axis_k in range(3):
        low_side, high_side = pairs[axis_k]
        flux_low, speed_low = flux_along(low_side, axis_k)
        flux_high, speed_high = flux_along(high_side, axis_k)
        flux_sum = flux_sum + 0.5 * (flux_high - flux_low)
        laplace = laplace + low_side + high_side
        gradient.append(0.5 * (speed_high - speed_low))
    vort_x = gradient[1][:, 2] - gradient[2][:, 1]
    vort_y = gradient[2][:, 0] - gradient[0][:, 2]
    vort_z = gradient[0][:, 1] - gradient[1][:, 0]
    lamb_vector = jnp.stack([
        vort_y * velocity[:, 2] - vort_z * velocity[:, 1],
        vort_z * velocity[:, 0] - vort_x * velocity[:, 2],
        vort_x * velocity[:, 1] - vort_y * velocity[:, 0],
    ], axis=1).astype(jnp.bfloat16)
    updated = conserved + DT_LES * (VISCOSITY * laplace - flux_sum)
    return updated, lamb_vector


def acoustic_advance(perturb, halo_cells, mean_state, source):
    pairs = neighbours(perturb, halo_cells)
    slopes = [0.5 * (high_side - low_side) for low_side, high_side in pairs]
    mean_density = mean_state[:, 0]
    mean_pressure = mean_state[:, 4]
    carried = mean_state[:, 1][:, None] * slopes[0] + mean_state[:, 2][:, None] * slopes[1] + mean_state[:, 3][:, None] * slopes[2]
    divergence = slopes[0][:, 1] + slopes[1][:, 2] + slopes[2][:, 3]
    members = [carried[:, 0] + mean_density * divergence]
    for axis_k in range(3):
        members.append(carried[:, 1 + axis_k] + slopes[axis_k][:, 4] / mean_density + source[:, axis_k])
    members.append(carried[:, 4] + 1.4 * mean_pressure * divergence)
    return perturb - DT_AC * jnp.stack(members, axis=1)


def invert_list(owner_list):
    count = owner_list.shape[0]
    return jnp.zeros((count,), jnp.int32).at[owner_list].set(jnp.arange(count, dtype=jnp.int32))


def halo_of(values, owner_list, partner_table):
    inverse = invert_list(owner_list)
    face_cells = face_layers(values)
    partner = partner_table[inverse]
    present = partner >= 0
    source_slot = owner_list[jnp.maximum(partner, 0)]
    opposite = jnp.array([1, 0, 3, 2, 5, 4], jnp.int32)
    picked = face_cells[source_slot, opposite[None, :]]
    return jnp.where(present[:, :, None, None], picked, face_cells)


def les_single(items):
    updated, lamb_vector = les_both(items[0][None], items[1][None])
    return updated[0], lamb_vector[0]


def acoustic_single(items):
    return acoustic_advance(items[0][None], items[1][None], items[2][None], items[3][None].astype(jnp.float32))[0]


def reference(state, mean_flow, les_owner, ac_owner, les_nbr, ac_nbr, coupling):
    inverse_ac = invert_list(ac_owner)
    coupled = les_owner[coupling[inverse_ac]]
    feed_slot = ac_owner[invert_list(coupling)[invert_list(les_owner)]]
    les_values = state[0]
    ac_values = state[1]
    for step_index in range(STEPS):
        les_halo = halo_of(les_values, les_owner, les_nbr)
        ac_halo = halo_of(ac_values, ac_owner, ac_nbr)
        back = ac_values[:, 1:4].astype(jnp.bfloat16)
        les_next, lamb_vector = lax.map(les_single, (les_values, les_halo))
        source = lamb_vector[coupled]
        feedback = back[feed_slot].astype(jnp.float32)
        ac_values = lax.map(acoustic_single, (ac_values, ac_halo, mean_flow, source))
        les_values = les_next.at[:, 1:4].add(DT_LES * FEEDBACK_GAIN * feedback)
    return jnp.stack([les_values, ac_values])
```

```python
import functools

import jax
import jax.numpy as jnp
from jax import lax
from jax.experimental import pallas as pl
from jax.experimental.pallas import tpu as pltpu
from jax.sharding import PartitionSpec as P

STEPS = 2
NB = 64
BS = 32
PAD = BS + 2
ROWS = PAD * 8
NCELL = 48
MESH = pl.DeviceIdType.MESH
F32 = jnp.float32
BF16 = jnp.bfloat16


def lookup(table, positions):
    hit = (positions[:, None] == lax.broadcasted_iota(jnp.int32, (1, NB), 1)).astype(jnp.int32)
    if table.ndim == 1:
        return jnp.sum(hit * table[None, :], axis=1)
    return jnp.sum(hit[:, :, None] * table[None], axis=1)


def invert(owner):
    slots = lax.broadcasted_iota(jnp.int32, (NB, NB), 0)
    blocks = lax.broadcasted_iota(jnp.int32, (NB, NB), 1)
    return jnp.sum(jnp.where(owner[None, :] == slots, blocks, 0), axis=1)


def make_tables(les_owner, ac_owner, les_nbr, ac_nbr, coupling):
    section = lax.axis_index("section")
    me = lax.axis_index("block")
    inv_les = invert(les_owner)
    inv_ac = invert(ac_owner)
    coupled = lookup(les_owner, lookup(coupling, inv_ac))
    feed = lookup(ac_owner, lookup(invert(coupling), inv_les))
    les_near = lookup(les_nbr, inv_les)
    ac_near = lookup(ac_nbr, inv_ac)
    cp_near = lookup(les_nbr, lookup(coupling, inv_ac))

    def slots_of(owner, near):
        return lookup(owner, near.reshape(-1)).reshape(NB, 6)

    axis_k = jnp.clip((me - NCELL) // 5, 0, 2)
    pick = lax.broadcasted_iota(jnp.int32, (1, 6), 1)

    def face(slots, d):
        return jnp.sum(jnp.where(pick == d, slots, 0), axis=1)

    own_slots = jnp.where(section == 0, slots_of(les_owner, les_near), slots_of(ac_owner, ac_near))
    cp_slots = slots_of(les_owner, cp_near)
    cells = jnp.where(section == 0, coupled, feed)
    is_cell = me < NCELL
    near = jnp.where(section == 0, les_near, ac_near)
    mine = lax.broadcasted_iota(jnp.int32, (NB, 1), 0) == me

    def flags(near):
        present = jnp.sum(jnp.where(mine, (near >= 0).astype(jnp.int32), 0), axis=0)
        return jnp.pad(present, (0, NB - 6))

    rows = [
        jnp.where(is_cell, cells, face(own_slots, 2 * axis_k)),
        jnp.where(is_cell, cells, face(own_slots, 2 * axis_k + 1)),
        face(cp_slots, 2 * axis_k),
        face(cp_slots, 2 * axis_k + 1),
        flags(near),
        flags(cp_near),
    ]
    return jnp.stack(rows, axis=0)


def kernel(tab, state_hbm, mean_hbm, out_hbm, q, acc, mean, ul, tile_a, recv_0, recv_1, sort_b, land, pick_ref,
           load_sem, loc_sem, sa, ra, sb, rb, rv, out_sem, side_sem):
    section = lax.axis_index("section")
    me = lax.axis_index("block")
    les = section == 0
    acoustic = section == 1
    q4 = q.reshape(5, PAD, 8, 128)
    acc4 = acc.reshape(5, BS, 8, 128)
    mean4 = mean.reshape(5, BS, 8, 128)

    def partner(n):
        return me ^ (n ^ 42)

    barrier = pltpu.get_barrier_semaphore()

    def greet(t, carry):
        pl.semaphore_signal(barrier, inc=1, device_id=(section, me ^ t), device_id_type=MESH)
        return carry

    pl.semaphore_signal(barrier, inc=1, device_id=(1 - section, me), device_id_type=MESH)
    lax.fori_loop(1, NB, greet, 0)

    recv_a = (recv_0, recv_1)

    def load_copy(c):
        return pltpu.make_async_copy(
            state_hbm.at[0, 0, :, :, pl.ds(128 * c, 128)], q4.at[:, pl.ds(1, BS), c, :], load_sem.at[0]
        )

    def mean_copy(c):
        return pltpu.make_async_copy(
            mean_hbm.at[0, :, :, pl.ds(128 * c, 128)], mean4.at[:, :, c, :], load_sem.at[1]
        )

    zero = jnp.zeros((8, 128), F32)
    for v in range(5):
        q[pl.ds(v * ROWS, 8), :] = zero
        q[pl.ds(v * ROWS + ROWS - 8, 8), :] = zero
    for c in range(8):
        load_copy(c).start()

    @pl.when(acoustic)
    def _():
        for c in range(8):
            mean_copy(c).start()

    lane = lax.broadcasted_iota(jnp.int32, (8, 128), 1)
    sub = lax.broadcasted_iota(jnp.int32, (8, 128), 0)
    zpos = lane % BS
    z_low = zpos == 0
    z_high = zpos == BS - 1
    even = lane % 2 == 0

    def up_y(v):
        r = pltpu.roll(v, 96, 1)
        return jnp.where(lane < 96, r, jnp.where(sub < 7, pltpu.roll(r, 7, 0), 0.0))

    def dn_y(v):
        r = pltpu.roll(v, 32, 1)
        return jnp.where(lane >= 32, r, jnp.where(sub > 0, pltpu.roll(r, 1, 0), 0.0))

    def up_z(v):
        return jnp.where(z_high, 0.0, pltpu.roll(v, 127, 1))

    def dn_z(v):
        return jnp.where(z_low, 0.0, pltpu.roll(v, 1, 1))

    lane_t = lax.broadcasted_iota(jnp.int32, (16, 128), 1)
    row_t = lax.broadcasted_iota(jnp.int32, (16, 128), 0)
    by_lane = jnp.where(lane_t % 2 == 1, 1.0, 0.0)
    by_row = jnp.where(row_t < 8, 1.0, 0.0)
    pick_ref[...] = jnp.where(me >= NCELL + 10, by_lane, by_row).astype(BF16)

    for s in range(STEPS):
        tile_a[s, NB - 1] = jnp.zeros((16, 128), BF16)
    loaded = q4.at[:, pl.ds(1, BS)]
    pltpu.make_async_copy(loaded, loaded, load_sem.at[0]).wait()

    def slab(v, x):
        return pl.ds(pl.multiple_of(v * ROWS + 8 * x + 8, 8), 8)

    def aslab(v, x):
        return pl.ds(pl.multiple_of(v * BS * 8 + 8 * x, 8), 8)

    @pl.when(les)
    def _():
        def prim(x, carry):
            inv = 1.0 / q[slab(0, x), :]
            for v in range(1, 4):
                q[slab(v, x), :] = q[slab(v, x), :] * inv
            return carry

        lax.fori_loop(0, BS, prim, 0, unroll=4)

    def pack(s):
        def cells(p, carry):
            for c in range(3):
                start = pl.multiple_of((c + 1) * ROWS + 16 * p + 8, 8)
                tile_a[s, c * 16 + p] = q[pl.ds(start, 16), :].astype(BF16)
            return carry

        lax.fori_loop(0, 16, cells, 0, unroll=4)

        def faces(v, carry):
            tile_a[s, NCELL + v] = jnp.concatenate(
                [q[slab(v, BS - 1), :], q[slab(v, 0), :]], axis=0
            ).astype(BF16)
            base = v * ROWS + 8
            low = high = zero
            for g in range(4):
                group = lane // 32 == g
                a = q[pl.ds(base + 64 * g, 8, stride=8), :]
                b = q[pl.ds(base + 64 * g + 7, 8, stride=8), :]
                low = jnp.where(group, a if g == 0 else pltpu.roll(a, 32 * g, 1), low)
                high = jnp.where(group, b if g == 3 else pltpu.roll(b, 32 * g + 32, 1), high)
            tile_a[s, NCELL + 5 + v] = jnp.concatenate([high, low], axis=0).astype(BF16)
            halves = []
            for half in range(2):
                packed = zero
                for x in range(16):
                    one = q[slab(v, 16 * half + x), :]
                    turned = one if x == 0 else pltpu.roll(one, 2 * x, 1)
                    packed = jnp.where(((lane + 1) % 32) // 2 == x, turned, packed)
                halves.append(packed)
            tile_a[s, NCELL + 10 + v] = jnp.concatenate(halves, axis=0).astype(BF16)
            return carry

        lax.fori_loop(0, 5, faces, 0)

    def send_a(s):
        def go(n, carry):
            j = partner(n)

            @pl.when(j != me)
            def _():
                pltpu.make_async_remote_copy(
                    src_ref=tile_a.at[s, j], dst_ref=recv_a[s].at[me], send_sem=sa.at[s], recv_sem=ra.at[s],
                    device_id=(section, j), device_id_type=MESH,
                ).start()

            @pl.when(j == me)
            def _():
                pltpu.make_async_copy(tile_a.at[s, me], recv_a[s].at[me], ra.at[s]).start()

            return carry

        lax.fori_loop(0, NB, go, 0)

    def les_terms(r, u, v, w, e, axis_k):
        vel = (u, v, w)
        m = (r * u, r * v, r * w)
        p = 0.4 * (e - 0.5 * (m[0] * u + m[1] * v + m[2] * w))
        speed = vel[axis_k]
        flux = [m[axis_k]] + [m[j] * speed + (p if j == axis_k else 0.0) for j in range(3)] + [(e + p) * speed]
        return (r,) + m + (e,), flux

    def les_interior():
        def body(x, carry):
            prev, plus = carry
            f = [q[slab(v, x), :] for v in range(5)]
            r, u, v_, w, e = f
            vel = (u, v_, w)
            m = (r * u, r * v_, r * w)
            p = 0.4 * (e - 0.5 * (m[0] * u + m[1] * v_ + m[2] * w))
            cons = (r,) + m + (e,)
            ep = e + p
            fluxes = []
            for k in range(3):
                sp = 0.1 * vel[k]
                fl = [0.1 * m[k]]
                for j in range(3):
                    t = m[j] * sp
                    if j == k:
                        t = t + 0.1 * p
                    fl.append(t)
                fl.append(ep * sp)
                fluxes.append(fl)
            new, nplus = [], []
            for i in range(5):
                d = 0.01 * cons[i]
                acc[aslab(i, jnp.maximum(x - 1, 0)), :] = prev[i] + (d - fluxes[0][i])
                total = 0.94 * cons[i] + plus[i]
                total = total + (up_y(d - fluxes[1][i]) + dn_y(d + fluxes[1][i]))
                total = total + (up_z(d - fluxes[2][i]) + dn_z(d + fluxes[2][i]))
                new.append(total)
                nplus.append(d + fluxes[0][i])
            return tuple(new), tuple(nplus)

        last, _ = lax.fori_loop(0, BS, body, ((zero,) * 5, (zero,) * 5))
        for i in range(5):
            acc[aslab(i, BS - 1), :] = last[i]

    def ac_interior():
        def body(x, carry):
            here = [q[slab(v, x), :] for v in range(5)]
            dx = [0.5 * (q[slab(v, x + 1), :] - q[slab(v, x - 1), :]) for v in range(5)]
            dy = [0.5 * (up_y(here[v]) - dn_y(here[v])) for v in range(5)]
            dz = [0.5 * (up_z(here[v]) - dn_z(here[v])) for v in range(5)]
            rho, wx, wy, wz, prs = [mean[aslab(v, x), :] for v in range(5)]
            inv = 1.0 / rho
            div = dx[1] + dy[2] + dz[3]
            adv = [wx * dx[v] + wy * dy[v] + wz * dz[v] for v in range(5)]
            extra = [rho * div, dx[4] * inv, dy[4] * inv, dz[4] * inv, (1.4 * prs) * div]
            for v in range(5):
                acc[aslab(v, x), :] = here[v] - 0.3 * (adv[v] + extra[v])
            return carry

        lax.fori_loop(0, BS, body, 0)

    def send_b(s):
        target = jnp.where(me < NCELL, 1 - section, section)
        face_id = me - NCELL
        axis_k = face_id // 5
        comp = face_id % 5 - 1
        tangential = les & (face_id >= 0) & (face_id < 15) & (comp >= 0) & (comp < 3) & (comp != axis_k)
        vel_slot = NB + jnp.maximum(2 * axis_k + comp - jnp.where(comp > axis_k, 1, 0), 0)
        from_low = pick_ref[...] > 0.5

        @pl.when(me != NB - 1)
        def _():
            def go(n, carry):
                dest = partner(n)
                sort_b[s, 0, dest] = jnp.where(from_low, recv_a[s][tab[0, dest]], recv_a[s][tab[1, dest]])
                local = (target == section) & (dest == me)

                @pl.when(jnp.logical_not(local))
                def _():
                    pltpu.make_async_remote_copy(
                        src_ref=sort_b.at[s, 0, dest], dst_ref=land.at[s, me], send_sem=sb.at[s],
                        recv_sem=rb.at[s], device_id=(target, dest), device_id_type=MESH,
                    ).start()

                @pl.when(local)
                def _():
                    pltpu.make_async_copy(sort_b.at[s, 0, dest], land.at[s, me], rb.at[s]).start()

                return carry

            lax.fori_loop(0, NB, go, 0)

        @pl.when(tangential)
        def _():
            def go(n, carry):
                dest = partner(n)
                sort_b[s, 1, dest] = jnp.where(from_low, recv_a[s][tab[2, dest]], recv_a[s][tab[3, dest]])
                pltpu.make_async_remote_copy(
                    src_ref=sort_b.at[s, 1, dest], dst_ref=land.at[s, vel_slot], send_sem=sb.at[STEPS + s],
                    recv_sem=rv.at[s], device_id=(1, dest), device_id_type=MESH,
                ).start()
                return carry

            lax.fori_loop(0, NB, go, 0)

        return tangential

    def tile(ref, *idx):
        return ref[idx].astype(F32)

    def halo_rows(s, axis_k, v):
        got = tile(land, s, NCELL + 5 * axis_k + v)
        own = tile(tile_a, s, NCELL + 5 * axis_k + v)
        low = jnp.where(tab[4, 2 * axis_k] > 0, got[:8], own[8:])
        high = jnp.where(tab[4, 2 * axis_k + 1] > 0, got[8:], own[:8])
        return low, high

    def turn_z(got, own, f_low, f_high):
        low = jnp.where(f_low > 0, pltpu.roll(got, 97, 1), own)
        high = jnp.where(f_high > 0, pltpu.roll(got, 31, 1), own)
        return jnp.where(even, low, high)

    def halo_z(s, v):
        got = tile(land, s, NCELL + 10 + v)
        own = tile(tile_a, s, NCELL + 10 + v)
        return [turn_z(got[8 * h:8 * h + 8], own[8 * h:8 * h + 8], tab[4, 4], tab[4, 5]) for h in range(2)]

    def les_finish(s, last):
        def side_terms(h, axis_k, sign):
            cons, flux = les_terms(*h, axis_k)
            return [0.01 * c + sign * f for c, f in zip(cons, flux)]

        pairs = [halo_rows(s, 0, v) for v in range(5)]
        for side, x, sign in ((0, 0, 0.1), (1, BS - 1, -0.1)):
            terms = side_terms([pr[side] for pr in pairs], 0, sign)
            for v in range(5):
                acc[aslab(v, x), :] = acc[aslab(v, x), :] + terms[v]
        pairs = [halo_rows(s, 1, v) for v in range(5)]
        for side, row, sign in ((0, 0, 0.1), (1, 7, -0.1)):
            terms = side_terms([pr[side] for pr in pairs], 1, sign)
            keep = lane < 32 if side == 0 else lane >= 96
            for v in range(5):
                for g in range(4):
                    amount = (128 - 32 * g if side == 0 else 96 - 32 * g) % 128
                    t = terms[v] if amount == 0 else pltpu.roll(terms[v], amount, 1)
                    where = pl.ds(v * BS * 8 + 64 * g + row, 8, stride=8)
                    acc[where, :] = acc[where, :] + jnp.where(keep, t, 0.0)
        zs = [halo_z(s, v) for v in range(5)]
        sign = jnp.where(even, 0.1, -0.1)
        edge = z_low | z_high
        for half in range(2):
            terms = side_terms([z[half] for z in zs], 2, sign)
            for p in range(8):
                back = [tile(land, s, c * 16 + 8 * half + p) for c in range(3)]
                for o in range(2):
                    x = 16 * half + 2 * p + o
                    new = []
                    for v in range(5):
                        amount = (128 - 2 * (2 * p + o)) % 128
                        t = terms[v] if amount == 0 else pltpu.roll(terms[v], amount, 1)
                        val = acc[aslab(v, x), :] + jnp.where(edge, t, 0.0)
                        if 1 <= v <= 3:
                            val = val + 0.1 * back[v - 1][8 * o:8 * o + 8]
                        new.append(val)
                    if not last:
                        inv = 1.0 / new[0]
                        new = [new[0]] + [new[v] * inv for v in range(1, 4)] + [new[4]]
                    for v in range(5):
                        q[slab(v, x), :] = new[v]

    def ac_finish(s):
        half_dt = 0.15
        UROWS = PAD * 8

        def uslab(c, x):
            return pl.ds(pl.multiple_of(c * UROWS + 8 * x + 8, 8), 8)

        def unpack(p, carry):
            for c in range(3):
                ul[pl.ds(pl.multiple_of(c * UROWS + 16 * p + 8, 8), 16), :] = tile(land, s, c * 16 + p)
            return carry

        lax.fori_loop(0, 16, unpack, 0, unroll=4)

        pairs = [halo_rows(s, 0, v) for v in range(5)]

        def side_terms(h, m, axis_k, alpha):
            rho, wx, wy, wz, prs = m
            w = (wx, wy, wz)[axis_k]
            terms = [w * h[v] for v in range(5)]
            terms[0] = terms[0] + rho * h[1 + axis_k]
            terms[1 + axis_k] = terms[1 + axis_k] + h[4] / rho
            terms[4] = terms[4] + (1.4 * prs) * h[1 + axis_k]
            return [alpha * t for t in terms]

        for side, x, alpha in ((0, 0, half_dt), (1, BS - 1, -half_dt)):
            m = [mean[aslab(v, x), :] for v in range(5)]
            terms = side_terms([pr[side] for pr in pairs], m, 0, alpha)
            for v in range(5):
                acc[aslab(v, x), :] = acc[aslab(v, x), :] + terms[v]
        pairs_y = [halo_rows(s, 1, v) for v in range(5)]
        zs = [halo_z(s, v) for v in range(5)]

        vel_count = land.at[s, pl.ds(NB, 6)]
        pltpu.make_async_copy(vel_count, vel_count, rv.at[s]).wait()

        vx = [tile(land, s, NB + o) for o in range(2)]
        for o, c in enumerate((1, 2)):
            ul[uslab(c, -1), :] = jnp.where(tab[5, 0] > 0, vx[o][:8], ul[uslab(c, 0), :])
            ul[uslab(c, BS), :] = jnp.where(tab[5, 1] > 0, vx[o][8:], ul[uslab(c, BS - 1), :])

        vy = [tile(land, s, NB + 2 + o) for o in range(2)]
        for side, row, alpha in ((0, 0, half_dt), (1, 7, -half_dt)):
            keep = lane < 32 if side == 0 else lane >= 96
            for g in range(4):
                amount = (128 - 32 * g if side == 0 else 96 - 32 * g) % 128

                def turned(t):
                    return t if amount == 0 else pltpu.roll(t, amount, 1)

                def strided(rows, v, lead):
                    return pl.ds(v * rows + lead + 64 * g + row, 8, stride=8)

                m = [mean[strided(BS * 8, v, 0), :] for v in range(5)]
                h = [turned(pr[side]) for pr in pairs_y]
                terms = side_terms(h, m, 1, alpha)
                u = [ul[strided(UROWS, c, 8), :] for c in range(3)]
                hx, hz = [
                    jnp.where(tab[5, 2 + side] > 0, turned(vy[o][8 * side:8 * side + 8]), u[c])
                    for o, c in enumerate((0, 2))
                ]
                terms[1] = terms[1] + alpha * (u[1] * hx)
                terms[2] = terms[2] - alpha * (hx * u[0] + hz * u[2])
                terms[3] = terms[3] + alpha * (u[1] * hz)
                for v in range(5):
                    where = strided(BS * 8, v, 0)
                    acc[where, :] = acc[where, :] + jnp.where(keep, terms[v], 0.0)

        vz = [tile(land, s, NB + 4 + o) for o in range(2)]
        edge = z_low | z_high
        alpha_z = jnp.where(z_low, half_dt, -half_dt)
        for half in range(2):
            for xx in range(16):
                x = 16 * half + xx
                amount = (128 - 2 * xx) % 128

                def turned(t):
                    return t if amount == 0 else pltpu.roll(t, amount, 1)

                m = [mean[aslab(v, x), :] for v in range(5)]
                h = [turned(zs[v][half]) for v in range(5)]
                terms = side_terms(h, m, 2, alpha_z)
                u = [ul[uslab(c, x), :] for c in range(3)]
                dxv, dxw = [0.5 * (ul[uslab(c, x + 1), :] - ul[uslab(c, x - 1), :]) for c in (1, 2)]
                dyu, dyw = [0.5 * (up_y(u[c]) - dn_y(u[c])) for c in (0, 2)]
                dz = []
                for o, c in enumerate((0, 1)):
                    got = vz[o][8 * half:8 * half + 8]
                    low = pltpu.roll(got, (97 + amount) % 128, 1)
                    high = pltpu.roll(got, (31 + amount) % 128, 1)
                    low = jnp.where(tab[5, 4] > 0, low, u[c])
                    high = jnp.where(tab[5, 5] > 0, high, u[c])
                    dz.append(0.5 * (jnp.where(z_high, high, pltpu.roll(u[c], 127, 1))
                                     - jnp.where(z_low, low, pltpu.roll(u[c], 1, 1))))
                dzu, dzv = dz
                ox, oy, oz = dyw - dzv, dzu - dxw, dxv - dyu
                lamb = (oy * u[2] - oz * u[1], oz * u[0] - ox * u[2], ox * u[1] - oy * u[0])
                for v in range(5):
                    val = acc[aslab(v, x), :] + jnp.where(edge, terms[v], 0.0)
                    if 1 <= v <= 3:
                        val = val - 0.3 * lamb[v - 1]
                    q[slab(v, x), :] = val

    pack(0)
    pl.semaphore_wait(barrier, NB)
    pl.semaphore_signal(side_sem, inc=1, device_id=(1 - section, me), device_id_type=MESH)
    send_a(0)

    @pl.when(acoustic)
    def _():
        pltpu.make_async_copy(mean4, mean4, load_sem.at[1]).wait()

    for s in range(STEPS):
        if s:
            pack(s)
            send_a(s)

        @pl.when(les)
        def _():
            les_interior()

        @pl.when(acoustic)
        def _():
            ac_interior()

        if s == 0:
            pl.semaphore_wait(side_sem, 1)
        pltpu.make_async_copy(recv_a[s], recv_a[s], ra.at[s]).wait()
        tangential = send_b(s)
        got = land.at[s, pl.ds(0, NB - 1)]
        pltpu.make_async_copy(got, got, rb.at[s]).wait()

        @pl.when(les)
        def _():
            les_finish(s, s == STEPS - 1)

        @pl.when(acoustic)
        def _():
            ac_finish(s)

    def out_copy(c):
        return pltpu.make_async_copy(
            q4.at[:, pl.ds(1, BS), c, :], out_hbm.at[0, 0, :, :, pl.ds(128 * c, 128)], out_sem
        )

    for c in range(8):
        out_copy(c).start()
    for s in range(STEPS):
        sent = tile_a.at[s, pl.ds(0, NB - 1)]
        pltpu.make_async_copy(sent, sent, sa.at[s]).wait()

        @pl.when(me != NB - 1)
        def _():
            everyone = sort_b.at[s, 0]
            others = sort_b.at[s, 0, pl.ds(0, NB - 1)]

            @pl.when(me < NCELL)
            def _():
                pltpu.make_async_copy(everyone, everyone, sb.at[s]).wait()

            @pl.when(me >= NCELL)
            def _():
                pltpu.make_async_copy(others, others, sb.at[s]).wait()

        @pl.when(tangential)
        def _():
            extra = sort_b.at[s, 1]
            pltpu.make_async_copy(extra, extra, sb.at[STEPS + s]).wait()

    final = q4.at[:, pl.ds(1, BS)]
    pltpu.make_async_copy(final, final, out_sem).wait()


def on_device(state, mean_flow, les_owner, ac_owner, les_nbr, ac_nbr, coupling):
    tables = make_tables(les_owner, ac_owner, les_nbr, ac_nbr, coupling)
    hbm = pl.BlockSpec(memory_space=pl.ANY)
    return pl.pallas_call(
        kernel,
        out_shape=jax.ShapeDtypeStruct(state.shape, F32),
        in_specs=[pl.BlockSpec(memory_space=pltpu.SMEM), hbm, hbm],
        out_specs=hbm,
        scratch_shapes=[
            pltpu.VMEM((5 * ROWS, 128), F32),
            pltpu.VMEM((5 * BS * 8, 128), F32),
            pltpu.VMEM((5 * BS * 8, 128), F32),
            pltpu.VMEM((3 * ROWS, 128), F32),
            pltpu.VMEM((STEPS, NB, 16, 128), BF16),
            pltpu.VMEM((NB, 16, 128), BF16),
            pltpu.VMEM((NB, 16, 128), BF16),
            pltpu.VMEM((STEPS, 2, NB, 16, 128), BF16),
            pltpu.VMEM((STEPS, NB + 6, 16, 128), BF16),
            pltpu.VMEM((16, 128), BF16),
            pltpu.SemaphoreType.DMA((2,)),
            pltpu.SemaphoreType.DMA((1,)),
            pltpu.SemaphoreType.DMA((STEPS,)),
            pltpu.SemaphoreType.DMA((STEPS,)),
            pltpu.SemaphoreType.DMA((2 * STEPS,)),
            pltpu.SemaphoreType.DMA((STEPS,)),
            pltpu.SemaphoreType.DMA((STEPS,)),
            pltpu.SemaphoreType.DMA(()),
            pltpu.SemaphoreType.REGULAR,
        ],
        compiler_params=pltpu.CompilerParams(
            collective_id=0, has_side_effects=True, vmem_limit_bytes=24 << 20
        ),
    )(tables, state, mean_flow)


def solution(mesh):
    placed = (P("section", "block"), P("block"), P(), P(), P(), P(), P())
    return jax.shard_map(
        on_device, mesh=mesh, in_specs=placed, out_specs=P("section", "block"), check_vma=False
    )
```

```python
import functools

import jax
import jax.numpy as jnp
from jax import lax
from jax.experimental import pallas as pl
from jax.experimental.pallas import tpu as pltpu
from jax.sharding import PartitionSpec as P

STEPS = 2
NB = 64
BS = 32
PAD = BS + 2
ROWS = PAD * 8
NCELL = 48
MESH = pl.DeviceIdType.MESH
F32 = jnp.float32
BF16 = jnp.bfloat16


def kernel(les_owner, ac_owner, coupling, les_nbr, ac_nbr, state_hbm, mean_hbm, out_ref, q, acc, mean, ul, tile_a, recv_0, recv_1, sort_b, land, pick_ref,
           list_0, list_1, list_2, near_0, near_1, idx_v, tab_v, tab, idx_sem, load_sem, tab_sem, sa, ra, sb, rb, rv, side_sem):
    section = lax.axis_index("section")
    me = lax.axis_index("block")
    les = section == 0
    acoustic = section == 1
    q4 = q.reshape(5, PAD, 8, 128)
    acc4 = acc.reshape(5, BS, 8, 128)
    mean4 = mean.reshape(5, BS, 8, 128)

    def partner(n):
        return me ^ (n ^ 42)

    barrier = pltpu.get_barrier_semaphore()

    def greet(n, carry):
        @pl.when(n != 42)
        def _():
            pl.semaphore_signal(barrier, inc=1, device_id=(section, partner(n)), device_id_type=MESH)

        return carry

    lax.fori_loop(0, NB, greet, 0)
    pl.semaphore_signal(barrier, inc=1, device_id=(1 - section, me), device_id_type=MESH)

    recv_a = (recv_0, recv_1)

    def load_copy(c):
        return pltpu.make_async_copy(
            state_hbm.at[0, 0, :, :, pl.ds(128 * c, 128)], q4.at[:, pl.ds(1, BS), c, :], load_sem.at[0]
        )

    def mean_copy(c):
        return pltpu.make_async_copy(
            mean_hbm.at[0, :, :, pl.ds(128 * c, 128)], mean4.at[:, :, c, :], load_sem.at[1]
        )

    zero = jnp.zeros((8, 128), F32)
    for v in range(5):
        q[pl.ds(v * ROWS, 8), :] = zero
        q[pl.ds(v * ROWS + ROWS - 8, 8), :] = zero
    for c in range(8):
        load_copy(c).start()
    lists = (list_0, list_1, list_2, near_0, near_1)
    idx_copies = [
        pltpu.make_async_copy(ref, lists[i], idx_sem.at[i])
        for i, ref in enumerate((les_owner, ac_owner, coupling, les_nbr, ac_nbr))
    ]
    for copy in idx_copies:
        copy.start()

    @pl.when(acoustic)
    def _():
        for c in range(8):
            mean_copy(c).start()

    lane = lax.broadcasted_iota(jnp.int32, (8, 128), 1)
    sub = lax.broadcasted_iota(jnp.int32, (8, 128), 0)
    zpos = lane % BS
    z_low = zpos == 0
    z_high = zpos == BS - 1
    even = lane % 2 == 0

    def up_y(v):
        r = pltpu.roll(v, 96, 1)
        return jnp.where(lane < 96, r, jnp.where(sub < 7, pltpu.roll(r, 7, 0), 0.0))

    def dn_y(v):
        r = pltpu.roll(v, 32, 1)
        return jnp.where(lane >= 32, r, jnp.where(sub > 0, pltpu.roll(r, 1, 0), 0.0))

    def up_z(v):
        return jnp.where(z_high, 0.0, pltpu.roll(v, 127, 1))

    def dn_z(v):
        return jnp.where(z_low, 0.0, pltpu.roll(v, 1, 1))

    lane_t = lax.broadcasted_iota(jnp.int32, (16, 128), 1)
    row_t = lax.broadcasted_iota(jnp.int32, (16, 128), 0)
    by_lane = jnp.where(lane_t % 2 == 1, 1.0, 0.0)
    by_row = jnp.where(row_t < 8, 1.0, 0.0)
    idx_v[...] = jnp.zeros((24, 128), jnp.int32)
    pick_ref[...] = jnp.where(me >= NCELL + 10, by_lane, by_row).astype(BF16)

    for s in range(STEPS):
        tile_a[s, NB - 1] = jnp.zeros((16, 128), BF16)
    loaded = q4.at[:, pl.ds(1, BS)]
    pltpu.make_async_copy(loaded, loaded, load_sem.at[0]).wait()

    def slab(v, x):
        return pl.ds(pl.multiple_of(v * ROWS + 8 * x + 8, 8), 8)

    def aslab(v, x):
        return pl.ds(pl.multiple_of(v * BS * 8 + 8 * x, 8), 8)

    @pl.when(les)
    def _():
        def prim(x, carry):
            inv = 1.0 / q[slab(0, x), :]
            for v in range(1, 4):
                q[slab(v, x), :] = q[slab(v, x), :] * inv
            return carry

        lax.fori_loop(0, BS, prim, 0, unroll=4)

    def make_tables():
        row = lax.broadcasted_iota(jnp.int32, (NB, 128), 0)
        col = lax.broadcasted_iota(jnp.int32, (NB, 128), 1)

        def over_lanes(a):
            for shift in (1, 2, 4, 8, 16, 32, 64):
                a = a + pltpu.roll(a, shift, 1)
            return a

        def over_rows(a):
            total = a[:8]
            for i in range(1, 8):
                total = total + a[8 * i:8 * i + 8]
            for shift in (1, 2, 4):
                total = total + pltpu.roll(total, shift, 0)
            return total

        def wide(a):
            return jnp.concatenate([a] * 8, axis=0)

        def column(i):
            line = jnp.broadcast_to(idx_v[pl.ds(i, 1), :], (NB, 128))
            return over_lanes(jnp.where(row == col, line, 0))

        def look(column_table, index_row):
            return over_rows(jnp.where(row == wide(index_row), column_table, 0))

        les_col, ac_col, link_col = column(0), column(1), column(2)
        own_col = jnp.where(les, les_col, ac_col)
        near_at = jnp.where(les, 8, 16)
        inv_own = over_rows(jnp.where(own_col == col, row, 0))
        inv_ac = over_rows(jnp.where(ac_col == col, row, 0))
        linked = look(link_col, inv_ac)
        coupled = look(les_col, linked)
        inv_les = over_rows(jnp.where(les_col == col, row, 0))
        feed = over_rows(jnp.where(link_col == wide(inv_les), ac_col, 0))
        cells = jnp.where(les, coupled, feed)
        axis_k = jnp.maximum(me - NCELL, 0) // 5
        rows = []
        for side in range(2):
            d = 2 * axis_k + side
            near_col = column(near_at + d)
            first = jnp.where(me < NCELL, cells, look(own_col, look(near_col, inv_own)))
            second = look(own_col, look(near_col, linked))
            rows.append((first, second))
        own_row = idx_v[pl.ds(jnp.where(les, 0, 1), 1), :]
        linked_me = over_rows(jnp.where(ac_col == me, link_col, 0))
        own_near = idx_v[pl.ds(pl.multiple_of(near_at, 8), 8), :]
        in_use = lane < NB
        mine = over_lanes(jnp.where((own_row == me) & in_use, own_near, 0))
        theirs = over_lanes(jnp.where((lane == linked_me) & in_use, idx_v[8:16, :], 0))
        out = jnp.zeros((8, 128), jnp.int32)
        for i, part in enumerate([rows[0][0], rows[1][0], rows[0][1], rows[1][1]]):
            out = jnp.where(sub == i, part, out)
        tab_v[0:8, :] = out
        tab_v[8:16, :] = mine
        tab_v[16:24, :] = theirs
        pltpu.make_async_copy(tab_v, tab, tab_sem).start()

    def pack(s):
        def cells(p, carry):
            for c in range(3):
                start = pl.multiple_of((c + 1) * ROWS + 16 * p + 8, 8)
                tile_a[s, c * 16 + p] = q[pl.ds(start, 16), :].astype(BF16)
            return carry

        lax.fori_loop(0, 16, cells, 0, unroll=4)

        def faces(v, carry):
            tile_a[s, NCELL + v] = jnp.concatenate(
                [q[slab(v, BS - 1), :], q[slab(v, 0), :]], axis=0
            ).astype(BF16)
            base = v * ROWS + 8
            low = high = zero
            for g in range(4):
                group = lane // 32 == g
                a = q[pl.ds(base + 64 * g, 8, stride=8), :]
                b = q[pl.ds(base + 64 * g + 7, 8, stride=8), :]
                low = jnp.where(group, a if g == 0 else pltpu.roll(a, 32 * g, 1), low)
                high = jnp.where(group, b if g == 3 else pltpu.roll(b, 32 * g + 32, 1), high)
            tile_a[s, NCELL + 5 + v] = jnp.concatenate([high, low], axis=0).astype(BF16)
            halves = []
            for half in range(2):
                packed = zero
                for x in range(16):
                    one = q[slab(v, 16 * half + x), :]
                    turned = one if x == 0 else pltpu.roll(one, 2 * x, 1)
                    packed = jnp.where(((lane + 1) % 32) // 2 == x, turned, packed)
                halves.append(packed)
            tile_a[s, NCELL + 10 + v] = jnp.concatenate(halves, axis=0).astype(BF16)
            return carry

        lax.fori_loop(0, 5, faces, 0)

    def send_a(s):
        def go(n, carry):
            j = partner(n)

            @pl.when(j != me)
            def _():
                pltpu.make_async_remote_copy(
                    src_ref=tile_a.at[s, j], dst_ref=recv_a[s].at[me], send_sem=sa.at[s], recv_sem=ra.at[s],
                    device_id=(section, j), device_id_type=MESH,
                ).start()

            @pl.when(j == me)
            def _():
                pltpu.make_async_copy(tile_a.at[s, me], recv_a[s].at[me], ra.at[s]).start()

            return carry

        lax.fori_loop(0, NB, go, 0)

    def put(v, x, value, last):
        if last:
            out_ref[pl.ds(v * BS * 8 + 64 * (x // 8) + x % 8, 8, stride=8), :] = value
        else:
            q[slab(v, x), :] = value

    def les_terms(r, u, v, w, e, axis_k):
        vel = (u, v, w)
        m = (r * u, r * v, r * w)
        p = 0.4 * (e - 0.5 * (m[0] * u + m[1] * v + m[2] * w))
        speed = vel[axis_k]
        flux = [m[axis_k]] + [m[j] * speed + (p if j == axis_k else 0.0) for j in range(3)] + [(e + p) * speed]
        return (r,) + m + (e,), flux

    def les_interior():
        def body(x, carry):
            prev, plus = carry
            f = [q[slab(v, x), :] for v in range(5)]
            r, u, v_, w, e = f
            vel = (u, v_, w)
            m = (r * u, r * v_, r * w)
            p = 0.4 * (e - 0.5 * (m[0] * u + m[1] * v_ + m[2] * w))
            cons = (r,) + m + (e,)
            ep = e + p
            fluxes = []
            for k in range(3):
                sp = 0.1 * vel[k]
                fl = [0.1 * m[k]]
                for j in range(3):
                    t = m[j] * sp
                    if j == k:
                        t = t + 0.1 * p
                    fl.append(t)
                fl.append(ep * sp)
                fluxes.append(fl)
            new, nplus = [], []
            for i in range(5):
                d = 0.01 * cons[i]
                acc[aslab(i, jnp.maximum(x - 1, 0)), :] = prev[i] + (d - fluxes[0][i])
                total = 0.94 * cons[i] + plus[i]
                total = total + (up_y(d - fluxes[1][i]) + dn_y(d + fluxes[1][i]))
                total = total + (up_z(d - fluxes[2][i]) + dn_z(d + fluxes[2][i]))
                new.append(total)
                nplus.append(d + fluxes[0][i])
            return tuple(new), tuple(nplus)

        last, _ = lax.fori_loop(0, BS, body, ((zero,) * 5, (zero,) * 5))
        for i in range(5):
            acc[aslab(i, BS - 1), :] = last[i]

    def ac_interior():
        def body(x, carry):
            here = [q[slab(v, x), :] for v in range(5)]
            dx = [0.5 * (q[slab(v, x + 1), :] - q[slab(v, x - 1), :]) for v in range(5)]
            dy = [0.5 * (up_y(here[v]) - dn_y(here[v])) for v in range(5)]
            dz = [0.5 * (up_z(here[v]) - dn_z(here[v])) for v in range(5)]
            rho, wx, wy, wz, prs = [mean[aslab(v, x), :] for v in range(5)]
            inv = 1.0 / rho
            div = dx[1] + dy[2] + dz[3]
            adv = [wx * dx[v] + wy * dy[v] + wz * dz[v] for v in range(5)]
            extra = [rho * div, dx[4] * inv, dy[4] * inv, dz[4] * inv, (1.4 * prs) * div]
            for v in range(5):
                acc[aslab(v, x), :] = here[v] - 0.3 * (adv[v] + extra[v])
            return carry

        lax.fori_loop(0, BS, body, 0)

    def send_b(s):
        target = jnp.where(me < NCELL, 1 - section, section)
        face_id = me - NCELL
        axis_k = face_id // 5
        comp = face_id % 5 - 1
        tangential = les & (face_id >= 0) & (face_id < 15) & (comp >= 0) & (comp < 3) & (comp != axis_k)
        vel_slot = NB + jnp.maximum(2 * axis_k + comp - jnp.where(comp > axis_k, 1, 0), 0)
        from_low = pick_ref[...] > 0.5

        @pl.when(me != NB - 1)
        def _():
            def go(n, carry):
                dest = partner(n)
                sort_b[s, 0, dest] = jnp.where(from_low, recv_a[s][tab[0, dest]], recv_a[s][tab[1, dest]])
                local = (target == section) & (dest == me)

                @pl.when(jnp.logical_not(local))
                def _():
                    pltpu.make_async_remote_copy(
                        src_ref=sort_b.at[s, 0, dest], dst_ref=land.at[s, me], send_sem=sb.at[s],
                        recv_sem=rb.at[s], device_id=(target, dest), device_id_type=MESH,
                    ).start()

                @pl.when(local)
                def _():
                    pltpu.make_async_copy(sort_b.at[s, 0, dest], land.at[s, me], rb.at[s]).start()

                @pl.when(tangential)
                def _():
                    sort_b[s, 1, dest] = jnp.where(from_low, recv_a[s][tab[2, dest]], recv_a[s][tab[3, dest]])
                    pltpu.make_async_remote_copy(
                        src_ref=sort_b.at[s, 1, dest], dst_ref=land.at[s, vel_slot], send_sem=sb.at[STEPS + s],
                        recv_sem=rv.at[s], device_id=(1, dest), device_id_type=MESH,
                    ).start()

                return carry

            lax.fori_loop(0, NB, go, 0)

        return tangential

    def tile(ref, *idx):
        return ref[idx].astype(F32)

    def halo_rows(s, axis_k, v):
        got = tile(land, s, NCELL + 5 * axis_k + v)
        own = tile(tile_a, s, NCELL + 5 * axis_k + v)
        low = jnp.where(tab[8 + 2 * axis_k, 0] >= 0, got[:8], own[8:])
        high = jnp.where(tab[9 + 2 * axis_k, 0] >= 0, got[8:], own[:8])
        return low, high

    def turn_z(got, own, f_low, f_high):
        low = jnp.where(f_low >= 0, pltpu.roll(got, 97, 1), own)
        high = jnp.where(f_high >= 0, pltpu.roll(got, 31, 1), own)
        return jnp.where(even, low, high)

    def halo_z(s, v):
        got = tile(land, s, NCELL + 10 + v)
        own = tile(tile_a, s, NCELL + 10 + v)
        return [turn_z(got[8 * h:8 * h + 8], own[8 * h:8 * h + 8], tab[12, 0], tab[13, 0]) for h in range(2)]

    def les_finish(s, last):
        def side_terms(h, axis_k, sign):
            cons, flux = les_terms(*h, axis_k)
            return [0.01 * c + sign * f for c, f in zip(cons, flux)]

        pairs = [halo_rows(s, 0, v) for v in range(5)]
        for side, x, sign in ((0, 0, 0.1), (1, BS - 1, -0.1)):
            terms = side_terms([pr[side] for pr in pairs], 0, sign)
            for v in range(5):
                acc[aslab(v, x), :] = acc[aslab(v, x), :] + terms[v]
        pairs = [halo_rows(s, 1, v) for v in range(5)]
        for side, row, sign in ((0, 0, 0.1), (1, 7, -0.1)):
            terms = side_terms([pr[side] for pr in pairs], 1, sign)
            keep = lane < 32 if side == 0 else lane >= 96
            for v in range(5):
                for g in range(4):
                    amount = (128 - 32 * g if side == 0 else 96 - 32 * g) % 128
                    t = terms[v] if amount == 0 else pltpu.roll(terms[v], amount, 1)
                    where = pl.ds(v * BS * 8 + 64 * g + row, 8, stride=8)
                    acc[where, :] = acc[where, :] + jnp.where(keep, t, 0.0)
        zs = [halo_z(s, v) for v in range(5)]
        sign = jnp.where(even, 0.1, -0.1)
        edge = z_low | z_high
        for half in range(2):
            terms = side_terms([z[half] for z in zs], 2, sign)
            for p in range(8):
                back = [tile(land, s, c * 16 + 8 * half + p) for c in range(3)]
                for o in range(2):
                    x = 16 * half + 2 * p + o
                    new = []
                    for v in range(5):
                        amount = (128 - 2 * (2 * p + o)) % 128
                        t = terms[v] if amount == 0 else pltpu.roll(terms[v], amount, 1)
                        val = acc[aslab(v, x), :] + jnp.where(edge, t, 0.0)
                        if 1 <= v <= 3:
                            val = val + 0.1 * back[v - 1][8 * o:8 * o + 8]
                        new.append(val)
                    if not last:
                        inv = 1.0 / new[0]
                        new = [new[0]] + [new[v] * inv for v in range(1, 4)] + [new[4]]
                    for v in range(5):
                        put(v, x, new[v], last)

    def ac_finish(s, last):
        half_dt = 0.15
        UROWS = PAD * 8

        def uslab(c, x):
            return pl.ds(pl.multiple_of(c * UROWS + 8 * x + 8, 8), 8)

        def unpack(p, carry):
            for c in range(3):
                ul[pl.ds(pl.multiple_of(c * UROWS + 16 * p + 8, 8), 16), :] = tile(land, s, c * 16 + p)
            return carry

        lax.fori_loop(0, 16, unpack, 0, unroll=4)

        pairs = [halo_rows(s, 0, v) for v in range(5)]

        def side_terms(h, m, axis_k, alpha):
            rho, wx, wy, wz, prs = m
            w = (wx, wy, wz)[axis_k]
            terms = [w * h[v] for v in range(5)]
            terms[0] = terms[0] + rho * h[1 + axis_k]
            terms[1 + axis_k] = terms[1 + axis_k] + h[4] / rho
            terms[4] = terms[4] + (1.4 * prs) * h[1 + axis_k]
            return [alpha * t for t in terms]

        for side, x, alpha in ((0, 0, half_dt), (1, BS - 1, -half_dt)):
            m = [mean[aslab(v, x), :] for v in range(5)]
            terms = side_terms([pr[side] for pr in pairs], m, 0, alpha)
            for v in range(5):
                acc[aslab(v, x), :] = acc[aslab(v, x), :] + terms[v]
        pairs_y = [halo_rows(s, 1, v) for v in range(5)]
        zs = [halo_z(s, v) for v in range(5)]

        vel_count = land.at[s, pl.ds(NB, 6)]
        pltpu.make_async_copy(vel_count, vel_count, rv.at[s]).wait()

        vx = [tile(land, s, NB + o) for o in range(2)]
        for o, c in enumerate((1, 2)):
            ul[uslab(c, -1), :] = jnp.where(tab[16, 0] >= 0, vx[o][:8], ul[uslab(c, 0), :])
            ul[uslab(c, BS), :] = jnp.where(tab[17, 0] >= 0, vx[o][8:], ul[uslab(c, BS - 1), :])

        vy = [tile(land, s, NB + 2 + o) for o in range(2)]
        for side, row, alpha in ((0, 0, half_dt), (1, 7, -half_dt)):
            keep = lane < 32 if side == 0 else lane >= 96
            for g in range(4):
                amount = (128 - 32 * g if side == 0 else 96 - 32 * g) % 128

                def turned(t):
                    return t if amount == 0 else pltpu.roll(t, amount, 1)

                def strided(rows, v, lead):
                    return pl.ds(v * rows + lead + 64 * g + row, 8, stride=8)

                m = [mean[strided(BS * 8, v, 0), :] for v in range(5)]
                h = [turned(pr[side]) for pr in pairs_y]
                terms = side_terms(h, m, 1, alpha)
                u = [ul[strided(UROWS, c, 8), :] for c in range(3)]
                hx, hz = [
                    jnp.where(tab[18 + side, 0] >= 0, turned(vy[o][8 * side:8 * side + 8]), u[c])
                    for o, c in enumerate((0, 2))
                ]
                terms[1] = terms[1] + alpha * (u[1] * hx)
                terms[2] = terms[2] - alpha * (hx * u[0] + hz * u[2])
                terms[3] = terms[3] + alpha * (u[1] * hz)
                for v in range(5):
                    where = strided(BS * 8, v, 0)
                    acc[where, :] = acc[where, :] + jnp.where(keep, terms[v], 0.0)

        vz = [tile(land, s, NB + 4 + o) for o in range(2)]
        edge = z_low | z_high
        alpha_z = jnp.where(z_low, half_dt, -half_dt)
        for half in range(2):
            for xx in range(16):
                x = 16 * half + xx
                amount = (128 - 2 * xx) % 128

                def turned(t):
                    return t if amount == 0 else pltpu.roll(t, amount, 1)

                m = [mean[aslab(v, x), :] for v in range(5)]
                h = [turned(zs[v][half]) for v in range(5)]
                terms = side_terms(h, m, 2, alpha_z)
                u = [ul[uslab(c, x), :] for c in range(3)]
                dxv, dxw = [0.5 * (ul[uslab(c, x + 1), :] - ul[uslab(c, x - 1), :]) for c in (1, 2)]
                dyu, dyw = [0.5 * (up_y(u[c]) - dn_y(u[c])) for c in (0, 2)]
                dz = []
                for o, c in enumerate((0, 1)):
                    got = vz[o][8 * half:8 * half + 8]
                    low = pltpu.roll(got, (97 + amount) % 128, 1)
                    high = pltpu.roll(got, (31 + amount) % 128, 1)
                    low = jnp.where(tab[20, 0] >= 0, low, u[c])
                    high = jnp.where(tab[21, 0] >= 0, high, u[c])
                    dz.append(0.5 * (jnp.where(z_high, high, pltpu.roll(u[c], 127, 1))
                                     - jnp.where(z_low, low, pltpu.roll(u[c], 1, 1))))
                dzu, dzv = dz
                ox, oy, oz = dyw - dzv, dzu - dxw, dxv - dyu
                lamb = (oy * u[2] - oz * u[1], oz * u[0] - ox * u[2], ox * u[1] - oy * u[0])
                for v in range(5):
                    val = acc[aslab(v, x), :] + jnp.where(edge, terms[v], 0.0)
                    if 1 <= v <= 3:
                        val = val - 0.3 * lamb[v - 1]
                    put(v, x, val, last)

    pack(0)
    pl.semaphore_wait(barrier, NB)
    pl.semaphore_signal(side_sem, inc=1, device_id=(1 - section, me), device_id_type=MESH)
    send_a(0)

    @pl.when(acoustic)
    def _():
        pltpu.make_async_copy(mean4, mean4, load_sem.at[1]).wait()

    for copy in idx_copies:
        copy.wait()
    for i in range(3):
        idx_v[pl.ds(i, 1), pl.ds(0, NB)] = lists[i][...]
    for i in range(2):
        idx_v[pl.ds(8 + 8 * i, 6), pl.ds(0, NB)] = lists[3 + i][...]
    make_tables()
    for s in range(STEPS):
        if s:
            pack(s)
            send_a(s)

        @pl.when(les)
        def _():
            les_interior()

        @pl.when(acoustic)
        def _():
            ac_interior()

        if s == 0:
            pl.semaphore_wait(side_sem, 1)
            pltpu.make_async_copy(tab_v, tab, tab_sem).wait()
        pltpu.make_async_copy(recv_a[s], recv_a[s], ra.at[s]).wait()
        tangential = send_b(s)
        got = land.at[s, pl.ds(0, NB - 1)]
        pltpu.make_async_copy(got, got, rb.at[s]).wait()

        @pl.when(les)
        def _():
            les_finish(s, s == STEPS - 1)

        @pl.when(acoustic)
        def _():
            ac_finish(s, s == STEPS - 1)

    for s in range(STEPS):
        sent = tile_a.at[s, pl.ds(0, NB - 1)]
        pltpu.make_async_copy(sent, sent, sa.at[s]).wait()

        @pl.when(me != NB - 1)
        def _():
            everyone = sort_b.at[s, 0]
            others = sort_b.at[s, 0, pl.ds(0, NB - 1)]

            @pl.when(me < NCELL)
            def _():
                pltpu.make_async_copy(everyone, everyone, sb.at[s]).wait()

            @pl.when(me >= NCELL)
            def _():
                pltpu.make_async_copy(others, others, sb.at[s]).wait()

        @pl.when(tangential)
        def _():
            extra = sort_b.at[s, 1]
            pltpu.make_async_copy(extra, extra, sb.at[STEPS + s]).wait()


def on_device(state, mean_flow, les_owner, ac_owner, les_nbr, ac_nbr, coupling):
    hbm = pl.BlockSpec(memory_space=pltpu.HBM)
    rows = pl.pallas_call(
        kernel,
        out_shape=pltpu.VMEM((5 * BS * 8, 128), F32),
        in_specs=[hbm] * 7,
        out_specs=pl.BlockSpec(memory_space=pltpu.VMEM),
        scratch_shapes=[
            pltpu.VMEM((5 * ROWS, 128), F32),
            pltpu.VMEM((5 * BS * 8, 128), F32),
            pltpu.VMEM((5 * BS * 8, 128), F32),
            pltpu.VMEM((3 * ROWS, 128), F32),
            pltpu.VMEM((STEPS, NB, 16, 128), BF16),
            pltpu.VMEM((NB, 16, 128), BF16),
            pltpu.VMEM((NB, 16, 128), BF16),
            pltpu.VMEM((STEPS, 2, NB, 16, 128), BF16),
            pltpu.VMEM((STEPS, NB + 6, 16, 128), BF16),
            pltpu.VMEM((16, 128), BF16),
            pltpu.VMEM((1, NB), jnp.int32),
            pltpu.VMEM((1, NB), jnp.int32),
            pltpu.VMEM((1, NB), jnp.int32),
            pltpu.VMEM((6, NB), jnp.int32),
            pltpu.VMEM((6, NB), jnp.int32),
            pltpu.VMEM((24, 128), jnp.int32),
            pltpu.VMEM((24, 128), jnp.int32),
            pltpu.SMEM((24, 128), jnp.int32),
            pltpu.SemaphoreType.DMA((5,)),
            pltpu.SemaphoreType.DMA((2,)),
            pltpu.SemaphoreType.DMA(()),
            pltpu.SemaphoreType.DMA((STEPS,)),
            pltpu.SemaphoreType.DMA((STEPS,)),
            pltpu.SemaphoreType.DMA((2 * STEPS,)),
            pltpu.SemaphoreType.DMA((STEPS,)),
            pltpu.SemaphoreType.DMA((STEPS,)),
            pltpu.SemaphoreType.REGULAR,
        ],
        compiler_params=pltpu.CompilerParams(
            collective_id=0, has_side_effects=True, vmem_limit_bytes=60 << 20
        ),
    )(les_owner[None], ac_owner[None], coupling[None], les_nbr.T, ac_nbr.T, state, mean_flow)
    tiles = rows.reshape(5, BS // 8, 8, 8, 128).transpose(0, 1, 3, 2, 4)
    return tiles.reshape(state.shape)


def solution(mesh):
    placed = (P("section", "block"), P("block"), P(), P(), P(), P(), P())
    return jax.shard_map(
        on_device, mesh=mesh, in_specs=placed, out_specs=P("section", "block"), check_vma=False
    )
```

```python
import functools

import jax
import jax.numpy as jnp
from jax import lax
from jax.experimental import pallas as pl
from jax.experimental.pallas import tpu as pltpu
from jax.sharding import PartitionSpec as P

STEPS = 2
NB = 64
BS = 32
PAD = BS + 2
ROWS = PAD * 8
NCELL = 48
MESH = pl.DeviceIdType.MESH
F32 = jnp.float32
BF16 = jnp.bfloat16


def kernel(les_owner, ac_owner, coupling, les_nbr, ac_nbr, state_hbm, mean_hbm, out_ref, q, acc, mean, ul, tile_a, recv_0, recv_1, sort_b, land, pick_ref,
           list_0, list_1, list_2, near_0, near_1, idx_v, tab_v, tab, idx_sem, load_sem, tab_sem, sa, ra, sb, rb, rv, side_sem):
    section = lax.axis_index("section")
    me = lax.axis_index("block")
    les = section == 0
    acoustic = section == 1
    q4 = q.reshape(5, PAD, 8, 128)
    acc4 = acc.reshape(5, BS, 8, 128)
    mean4 = mean.reshape(5, BS, 8, 128)

    def partner(n):
        return me ^ (n ^ 42)

    barrier = pltpu.get_barrier_semaphore()

    def greet(n, carry):
        @pl.when(n != 42)
        def _():
            pl.semaphore_signal(barrier, inc=1, device_id=(section, partner(n)), device_id_type=MESH)

        return carry

    lax.fori_loop(0, NB, greet, 0)
    pl.semaphore_signal(barrier, inc=1, device_id=(1 - section, me), device_id_type=MESH)

    recv_a = (recv_0, recv_1)

    def load_copy(c):
        return pltpu.make_async_copy(
            state_hbm.at[0, 0, :, :, pl.ds(128 * c, 128)], q4.at[:, pl.ds(1, BS), c, :], load_sem.at[0]
        )

    def mean_copy(c):
        return pltpu.make_async_copy(
            mean_hbm.at[0, :, :, pl.ds(128 * c, 128)], mean4.at[:, :, c, :], load_sem.at[1]
        )

    zero = jnp.zeros((8, 128), F32)
    for v in range(5):
        q[pl.ds(v * ROWS, 8), :] = zero
        q[pl.ds(v * ROWS + ROWS - 8, 8), :] = zero
    for c in range(8):
        load_copy(c).start()
    lists = (list_0, list_1, list_2, near_0, near_1)
    idx_copies = [
        pltpu.make_async_copy(ref, lists[i], idx_sem.at[i])
        for i, ref in enumerate((les_owner, ac_owner, coupling, les_nbr, ac_nbr))
    ]
    for copy in idx_copies:
        copy.start()

    @pl.when(acoustic)
    def _():
        for c in range(8):
            mean_copy(c).start()

    lane = lax.broadcasted_iota(jnp.int32, (8, 128), 1)
    sub = lax.broadcasted_iota(jnp.int32, (8, 128), 0)
    zpos = lane % BS
    z_low = zpos == 0
    z_high = zpos == BS - 1
    even = lane % 2 == 0

    def up_y(v):
        r = pltpu.roll(v, 96, 1)
        return jnp.where(lane < 96, r, jnp.where(sub < 7, pltpu.roll(r, 7, 0), 0.0))

    def dn_y(v):
        r = pltpu.roll(v, 32, 1)
        return jnp.where(lane >= 32, r, jnp.where(sub > 0, pltpu.roll(r, 1, 0), 0.0))

    def up_z(v):
        return jnp.where(z_high, 0.0, pltpu.roll(v, 127, 1))

    def dn_z(v):
        return jnp.where(z_low, 0.0, pltpu.roll(v, 1, 1))

    lane_t = lax.broadcasted_iota(jnp.int32, (16, 128), 1)
    row_t = lax.broadcasted_iota(jnp.int32, (16, 128), 0)
    by_lane = jnp.where(lane_t % 2 == 1, 1.0, 0.0)
    by_row = jnp.where(row_t < 8, 1.0, 0.0)
    idx_v[...] = jnp.zeros((24, 128), jnp.int32)
    pick_ref[...] = jnp.where(me >= NCELL + 10, by_lane, by_row).astype(BF16)

    for s in range(STEPS):
        tile_a[s, NB - 1] = jnp.zeros((16, 128), BF16)
    loaded = q4.at[:, pl.ds(1, BS)]
    pltpu.make_async_copy(loaded, loaded, load_sem.at[0]).wait()

    def slab(v, x):
        return pl.ds(pl.multiple_of(v * ROWS + 8 * x + 8, 8), 8)

    def aslab(v, x):
        return pl.ds(pl.multiple_of(v * BS * 8 + 8 * x, 8), 8)

    @pl.when(les)
    def _():
        def prim(x, carry):
            inv = 1.0 / q[slab(0, x), :]
            for v in range(1, 4):
                q[slab(v, x), :] = q[slab(v, x), :] * inv
            return carry

        lax.fori_loop(0, BS, prim, 0, unroll=4)

    def make_tables():
        row = lax.broadcasted_iota(jnp.int32, (NB, 128), 0)
        col = lax.broadcasted_iota(jnp.int32, (NB, 128), 1)

        def over_lanes(a):
            for shift in (1, 2, 4, 8, 16, 32, 64):
                a = a + pltpu.roll(a, shift, 1)
            return a

        def over_rows(a):
            total = a[:8]
            for i in range(1, 8):
                total = total + a[8 * i:8 * i + 8]
            for shift in (1, 2, 4):
                total = total + pltpu.roll(total, shift, 0)
            return total

        def wide(a):
            return jnp.concatenate([a] * 8, axis=0)

        def column(i):
            line = jnp.broadcast_to(idx_v[pl.ds(i, 1), :], (NB, 128))
            return over_lanes(jnp.where(row == col, line, 0))

        def look(column_table, index_row):
            return over_rows(jnp.where(row == wide(index_row), column_table, 0))

        les_col, ac_col, link_col = column(0), column(1), column(2)
        own_col = jnp.where(les, les_col, ac_col)
        near_at = jnp.where(les, 8, 16)
        inv_own = over_rows(jnp.where(own_col == col, row, 0))
        inv_ac = over_rows(jnp.where(ac_col == col, row, 0))
        linked = look(link_col, inv_ac)
        coupled = look(les_col, linked)
        inv_les = over_rows(jnp.where(les_col == col, row, 0))
        feed = over_rows(jnp.where(link_col == wide(inv_les), ac_col, 0))
        cells = jnp.where(les, coupled, feed)
        axis_k = jnp.maximum(me - NCELL, 0) // 5
        rows = []
        for side in range(2):
            d = 2 * axis_k + side
            near_col = column(near_at + d)
            first = jnp.where(me < NCELL, cells, look(own_col, look(near_col, inv_own)))
            second = look(own_col, look(near_col, linked))
            rows.append((first, second))
        own_row = idx_v[pl.ds(jnp.where(les, 0, 1), 1), :]
        linked_me = over_rows(jnp.where(ac_col == me, link_col, 0))
        own_near = idx_v[pl.ds(pl.multiple_of(near_at, 8), 8), :]
        in_use = lane < NB
        mine = over_lanes(jnp.where((own_row == me) & in_use, own_near, 0))
        theirs = over_lanes(jnp.where((lane == linked_me) & in_use, idx_v[8:16, :], 0))
        out = jnp.zeros((8, 128), jnp.int32)
        for i, part in enumerate([rows[0][0], rows[1][0], rows[0][1], rows[1][1]]):
            out = jnp.where(sub == i, part, out)
        tab_v[0:8, :] = out
        tab_v[8:16, :] = mine
        tab_v[16:24, :] = theirs
        pltpu.make_async_copy(tab_v, tab, tab_sem).start()

    def pack(s):
        def cells(p, carry):
            for c in range(3):
                start = pl.multiple_of((c + 1) * ROWS + 16 * p + 8, 8)
                tile_a[s, c * 16 + p] = q[pl.ds(start, 16), :].astype(BF16)
            return carry

        lax.fori_loop(0, 16, cells, 0, unroll=4)

        def faces(v, carry):
            tile_a[s, NCELL + v] = jnp.concatenate(
                [q[slab(v, BS - 1), :], q[slab(v, 0), :]], axis=0
            ).astype(BF16)
            base = v * ROWS + 8
            low = high = zero
            for g in range(4):
                group = lane // 32 == g
                a = q[pl.ds(base + 64 * g, 8, stride=8), :]
                b = q[pl.ds(base + 64 * g + 7, 8, stride=8), :]
                low = jnp.where(group, a if g == 0 else pltpu.roll(a, 32 * g, 1), low)
                high = jnp.where(group, b if g == 3 else pltpu.roll(b, 32 * g + 32, 1), high)
            tile_a[s, NCELL + 5 + v] = jnp.concatenate([high, low], axis=0).astype(BF16)
            halves = []
            for half in range(2):
                packed = zero
                for x in range(16):
                    one = q[slab(v, 16 * half + x), :]
                    turned = one if x == 0 else pltpu.roll(one, 2 * x, 1)
                    packed = jnp.where(((lane + 1) % 32) // 2 == x, turned, packed)
                halves.append(packed)
            tile_a[s, NCELL + 10 + v] = jnp.concatenate(halves, axis=0).astype(BF16)
            return carry

        lax.fori_loop(0, 5, faces, 0)

    def others(go, unroll):
        lax.fori_loop(0, 42, go, 0, unroll=unroll)
        lax.fori_loop(43, NB, go, 0, unroll=unroll)

    def send_a(s):
        def go(n, carry):
            j = partner(n)
            pltpu.make_async_remote_copy(
                src_ref=tile_a.at[s, j], dst_ref=recv_a[s].at[me], send_sem=sa.at[s], recv_sem=ra.at[s],
                device_id=(section, j), device_id_type=MESH,
            ).start()
            return carry

        others(go, 1)
        pltpu.make_async_copy(tile_a.at[s, me], recv_a[s].at[me], ra.at[s]).start()

    def put(v, x, value, last):
        if last:
            out_ref[pl.ds(v * BS * 8 + 64 * (x // 8) + x % 8, 8, stride=8), :] = value
        else:
            q[slab(v, x), :] = value

    def les_terms(r, u, v, w, e, axis_k):
        vel = (u, v, w)
        m = (r * u, r * v, r * w)
        p = 0.4 * (e - 0.5 * (m[0] * u + m[1] * v + m[2] * w))
        speed = vel[axis_k]
        flux = [m[axis_k]] + [m[j] * speed + (p if j == axis_k else 0.0) for j in range(3)] + [(e + p) * speed]
        return (r,) + m + (e,), flux

    def les_interior():
        def body(x, carry):
            prev, plus = carry
            f = [q[slab(v, x), :] for v in range(5)]
            r, u, v_, w, e = f
            vel = (u, v_, w)
            m = (r * u, r * v_, r * w)
            p = 0.4 * (e - 0.5 * (m[0] * u + m[1] * v_ + m[2] * w))
            cons = (r,) + m + (e,)
            ep = e + p
            fluxes = []
            for k in range(3):
                sp = 0.1 * vel[k]
                fl = [0.1 * m[k]]
                for j in range(3):
                    t = m[j] * sp
                    if j == k:
                        t = t + 0.1 * p
                    fl.append(t)
                fl.append(ep * sp)
                fluxes.append(fl)
            new, nplus = [], []
            for i in range(5):
                d = 0.01 * cons[i]
                acc[aslab(i, jnp.maximum(x - 1, 0)), :] = prev[i] + (d - fluxes[0][i])
                total = 0.94 * cons[i] + plus[i]
                total = total + (up_y(d - fluxes[1][i]) + dn_y(d + fluxes[1][i]))
                total = total + (up_z(d - fluxes[2][i]) + dn_z(d + fluxes[2][i]))
                new.append(total)
                nplus.append(d + fluxes[0][i])
            return tuple(new), tuple(nplus)

        last, _ = lax.fori_loop(0, BS, body, ((zero,) * 5, (zero,) * 5))
        for i in range(5):
            acc[aslab(i, BS - 1), :] = last[i]

    def ac_interior():
        def body(x, carry):
            here = [q[slab(v, x), :] for v in range(5)]
            dx = [0.5 * (q[slab(v, x + 1), :] - q[slab(v, x - 1), :]) for v in range(5)]
            dy = [0.5 * (up_y(here[v]) - dn_y(here[v])) for v in range(5)]
            dz = [0.5 * (up_z(here[v]) - dn_z(here[v])) for v in range(5)]
            rho, wx, wy, wz, prs = [mean[aslab(v, x), :] for v in range(5)]
            inv = 1.0 / rho
            div = dx[1] + dy[2] + dz[3]
            adv = [wx * dx[v] + wy * dy[v] + wz * dz[v] for v in range(5)]
            extra = [rho * div, dx[4] * inv, dy[4] * inv, dz[4] * inv, (1.4 * prs) * div]
            for v in range(5):
                acc[aslab(v, x), :] = here[v] - 0.3 * (adv[v] + extra[v])
            return carry

        lax.fori_loop(0, BS, body, 0)

    def send_b(s):
        target = jnp.where(me < NCELL, 1 - section, section)
        face_id = me - NCELL
        axis_k = face_id // 5
        comp = face_id % 5 - 1
        tangential = les & (face_id >= 0) & (face_id < 15) & (comp >= 0) & (comp < 3) & (comp != axis_k)
        vel_slot = NB + jnp.maximum(2 * axis_k + comp - jnp.where(comp > axis_k, 1, 0), 0)
        from_low = pick_ref[...] > 0.5

        def join(slot, dest):
            low, high = recv_a[s][tab[2 * slot, dest]], recv_a[s][tab[2 * slot + 1, dest]]
            sort_b[s, slot, dest] = jnp.where(from_low, low, high)

        def send_main(dest):
            join(0, dest)
            pltpu.make_async_remote_copy(
                src_ref=sort_b.at[s, 0, dest], dst_ref=land.at[s, me], send_sem=sb.at[s],
                recv_sem=rb.at[s], device_id=(target, dest), device_id_type=MESH,
            ).start()

        def send_vel(dest):
            join(1, dest)
            pltpu.make_async_remote_copy(
                src_ref=sort_b.at[s, 1, dest], dst_ref=land.at[s, vel_slot], send_sem=sb.at[STEPS + s],
                recv_sem=rv.at[s], device_id=(1, dest), device_id_type=MESH,
            ).start()

        def go_main(n, carry):
            send_main(partner(n))
            return carry

        def go_vel(n, carry):
            send_vel(partner(n))
            return carry

        @pl.when((me != NB - 1) & jnp.logical_not(tangential))
        def _():
            others(go_main, 1)

            @pl.when(me < NCELL)
            def _():
                send_main(me)

        @pl.when(tangential)
        def _():
            others(go_vel, 1)
            send_vel(me)
            others(go_main, 1)

        @pl.when((me >= NCELL) & (me != NB - 1))
        def _():
            join(0, me)
            pltpu.make_async_copy(sort_b.at[s, 0, me], land.at[s, me], rb.at[s]).start()

        return tangential

    def tile(ref, *idx):
        return ref[idx].astype(F32)

    def halo_rows(s, axis_k, v):
        got = tile(land, s, NCELL + 5 * axis_k + v)
        own = tile(tile_a, s, NCELL + 5 * axis_k + v)
        low = jnp.where(tab[8 + 2 * axis_k, 0] >= 0, got[:8], own[8:])
        high = jnp.where(tab[9 + 2 * axis_k, 0] >= 0, got[8:], own[:8])
        return low, high

    def turn_z(got, own, f_low, f_high):
        low = jnp.where(f_low >= 0, pltpu.roll(got, 97, 1), own)
        high = jnp.where(f_high >= 0, pltpu.roll(got, 31, 1), own)
        return jnp.where(even, low, high)

    def halo_z(s, v):
        got = tile(land, s, NCELL + 10 + v)
        own = tile(tile_a, s, NCELL + 10 + v)
        return [turn_z(got[8 * h:8 * h + 8], own[8 * h:8 * h + 8], tab[12, 0], tab[13, 0]) for h in range(2)]

    def les_finish(s, last):
        def side_terms(h, axis_k, sign):
            cons, flux = les_terms(*h, axis_k)
            return [0.01 * c + sign * f for c, f in zip(cons, flux)]

        pairs = [halo_rows(s, 0, v) for v in range(5)]
        for side, x, sign in ((0, 0, 0.1), (1, BS - 1, -0.1)):
            terms = side_terms([pr[side] for pr in pairs], 0, sign)
            for v in range(5):
                acc[aslab(v, x), :] = acc[aslab(v, x), :] + terms[v]
        pairs = [halo_rows(s, 1, v) for v in range(5)]
        for side, row, sign in ((0, 0, 0.1), (1, 7, -0.1)):
            terms = side_terms([pr[side] for pr in pairs], 1, sign)
            keep = lane < 32 if side == 0 else lane >= 96
            for v in range(5):
                for g in range(4):
                    amount = (128 - 32 * g if side == 0 else 96 - 32 * g) % 128
                    t = terms[v] if amount == 0 else pltpu.roll(terms[v], amount, 1)
                    where = pl.ds(v * BS * 8 + 64 * g + row, 8, stride=8)
                    acc[where, :] = acc[where, :] + jnp.where(keep, t, 0.0)
        zs = [halo_z(s, v) for v in range(5)]
        sign = jnp.where(even, 0.1, -0.1)
        edge = z_low | z_high
        for half in range(2):
            terms = side_terms([z[half] for z in zs], 2, sign)
            for p in range(8):
                back = [tile(land, s, c * 16 + 8 * half + p) for c in range(3)]
                for o in range(2):
                    x = 16 * half + 2 * p + o
                    new = []
                    for v in range(5):
                        amount = (128 - 2 * (2 * p + o)) % 128
                        t = terms[v] if amount == 0 else pltpu.roll(terms[v], amount, 1)
                        val = acc[aslab(v, x), :] + jnp.where(edge, t, 0.0)
                        if 1 <= v <= 3:
                            val = val + 0.1 * back[v - 1][8 * o:8 * o + 8]
                        new.append(val)
                    if not last:
                        inv = 1.0 / new[0]
                        new = [new[0]] + [new[v] * inv for v in range(1, 4)] + [new[4]]
                    for v in range(5):
                        put(v, x, new[v], last)

    def ac_finish(s, last):
        half_dt = 0.15
        UROWS = PAD * 8

        def uslab(c, x):
            return pl.ds(pl.multiple_of(c * UROWS + 8 * x + 8, 8), 8)

        def unpack(p, carry):
            for c in range(3):
                ul[pl.ds(pl.multiple_of(c * UROWS + 16 * p + 8, 8), 16), :] = tile(land, s, c * 16 + p)
            return carry

        lax.fori_loop(0, 16, unpack, 0, unroll=4)

        pairs = [halo_rows(s, 0, v) for v in range(5)]

        def side_terms(h, m, axis_k, alpha):
            rho, wx, wy, wz, prs = m
            w = (wx, wy, wz)[axis_k]
            terms = [w * h[v] for v in range(5)]
            terms[0] = terms[0] + rho * h[1 + axis_k]
            terms[1 + axis_k] = terms[1 + axis_k] + h[4] / rho
            terms[4] = terms[4] + (1.4 * prs) * h[1 + axis_k]
            return [alpha * t for t in terms]

        for side, x, alpha in ((0, 0, half_dt), (1, BS - 1, -half_dt)):
            m = [mean[aslab(v, x), :] for v in range(5)]
            terms = side_terms([pr[side] for pr in pairs], m, 0, alpha)
            for v in range(5):
                acc[aslab(v, x), :] = acc[aslab(v, x), :] + terms[v]
        pairs_y = [halo_rows(s, 1, v) for v in range(5)]
        zs = [halo_z(s, v) for v in range(5)]

        vel_count = land.at[s, pl.ds(NB, 6)]
        pltpu.make_async_copy(vel_count, vel_count, rv.at[s]).wait()

        vx = [tile(land, s, NB + o) for o in range(2)]
        for o, c in enumerate((1, 2)):
            ul[uslab(c, -1), :] = jnp.where(tab[16, 0] >= 0, vx[o][:8], ul[uslab(c, 0), :])
            ul[uslab(c, BS), :] = jnp.where(tab[17, 0] >= 0, vx[o][8:], ul[uslab(c, BS - 1), :])

        vy = [tile(land, s, NB + 2 + o) for o in range(2)]
        for side, row, alpha in ((0, 0, half_dt), (1, 7, -half_dt)):
            keep = lane < 32 if side == 0 else lane >= 96
            for g in range(4):
                amount = (128 - 32 * g if side == 0 else 96 - 32 * g) % 128

                def turned(t):
                    return t if amount == 0 else pltpu.roll(t, amount, 1)

                def strided(rows, v, lead):
                    return pl.ds(v * rows + lead + 64 * g + row, 8, stride=8)

                m = [mean[strided(BS * 8, v, 0), :] for v in range(5)]
                h = [turned(pr[side]) for pr in pairs_y]
                terms = side_terms(h, m, 1, alpha)
                u = [ul[strided(UROWS, c, 8), :] for c in range(3)]
                hx, hz = [
                    jnp.where(tab[18 + side, 0] >= 0, turned(vy[o][8 * side:8 * side + 8]), u[c])
                    for o, c in enumerate((0, 2))
                ]
                terms[1] = terms[1] + alpha * (u[1] * hx)
                terms[2] = terms[2] - alpha * (hx * u[0] + hz * u[2])
                terms[3] = terms[3] + alpha * (u[1] * hz)
                for v in range(5):
                    where = strided(BS * 8, v, 0)
                    acc[where, :] = acc[where, :] + jnp.where(keep, terms[v], 0.0)

        vz = [tile(land, s, NB + 4 + o) for o in range(2)]
        edge = z_low | z_high
        alpha_z = jnp.where(z_low, half_dt, -half_dt)
        for half in range(2):
            for xx in range(16):
                x = 16 * half + xx
                amount = (128 - 2 * xx) % 128

                def turned(t):
                    return t if amount == 0 else pltpu.roll(t, amount, 1)

                m = [mean[aslab(v, x), :] for v in range(5)]
                h = [turned(zs[v][half]) for v in range(5)]
                terms = side_terms(h, m, 2, alpha_z)
                u = [ul[uslab(c, x), :] for c in range(3)]
                dxv, dxw = [0.5 * (ul[uslab(c, x + 1), :] - ul[uslab(c, x - 1), :]) for c in (1, 2)]
                dyu, dyw = [0.5 * (up_y(u[c]) - dn_y(u[c])) for c in (0, 2)]
                dz = []
                for o, c in enumerate((0, 1)):
                    got = vz[o][8 * half:8 * half + 8]
                    low = pltpu.roll(got, (97 + amount) % 128, 1)
                    high = pltpu.roll(got, (31 + amount) % 128, 1)
                    low = jnp.where(tab[20, 0] >= 0, low, u[c])
                    high = jnp.where(tab[21, 0] >= 0, high, u[c])
                    dz.append(0.5 * (jnp.where(z_high, high, pltpu.roll(u[c], 127, 1))
                                     - jnp.where(z_low, low, pltpu.roll(u[c], 1, 1))))
                dzu, dzv = dz
                ox, oy, oz = dyw - dzv, dzu - dxw, dxv - dyu
                lamb = (oy * u[2] - oz * u[1], oz * u[0] - ox * u[2], ox * u[1] - oy * u[0])
                for v in range(5):
                    val = acc[aslab(v, x), :] + jnp.where(edge, terms[v], 0.0)
                    if 1 <= v <= 3:
                        val = val - 0.3 * lamb[v - 1]
                    put(v, x, val, last)

    pack(0)
    pl.semaphore_wait(barrier, NB)
    pl.semaphore_signal(side_sem, inc=1, device_id=(1 - section, me), device_id_type=MESH)
    send_a(0)

    @pl.when(acoustic)
    def _():
        pltpu.make_async_copy(mean4, mean4, load_sem.at[1]).wait()

    for copy in idx_copies:
        copy.wait()
    for i in range(3):
        idx_v[pl.ds(i, 1), pl.ds(0, NB)] = lists[i][...]
    for i in range(2):
        idx_v[pl.ds(8 + 8 * i, 6), pl.ds(0, NB)] = lists[3 + i][...]
    make_tables()
    for s in range(STEPS):
        if s:
            pack(s)
            send_a(s)

        @pl.when(les)
        def _():
            les_interior()

        @pl.when(acoustic)
        def _():
            ac_interior()

        if s == 0:
            pl.semaphore_wait(side_sem, 1)
            pltpu.make_async_copy(tab_v, tab, tab_sem).wait()
        pltpu.make_async_copy(recv_a[s], recv_a[s], ra.at[s]).wait()
        tangential = send_b(s)
        got = land.at[s, pl.ds(0, NB - 1)]
        pltpu.make_async_copy(got, got, rb.at[s]).wait()

        @pl.when(les)
        def _():
            les_finish(s, s == STEPS - 1)

        @pl.when(acoustic)
        def _():
            ac_finish(s, s == STEPS - 1)

    for s in range(STEPS):
        sent = tile_a.at[s, pl.ds(0, NB - 1)]
        pltpu.make_async_copy(sent, sent, sa.at[s]).wait()

        @pl.when(me != NB - 1)
        def _():
            everyone = sort_b.at[s, 0]
            others = sort_b.at[s, 0, pl.ds(0, NB - 1)]

            @pl.when(me < NCELL)
            def _():
                pltpu.make_async_copy(everyone, everyone, sb.at[s]).wait()

            @pl.when(me >= NCELL)
            def _():
                pltpu.make_async_copy(others, others, sb.at[s]).wait()

        @pl.when(tangential)
        def _():
            extra = sort_b.at[s, 1]
            pltpu.make_async_copy(extra, extra, sb.at[STEPS + s]).wait()


def on_device(state, mean_flow, les_owner, ac_owner, les_nbr, ac_nbr, coupling):
    hbm = pl.BlockSpec(memory_space=pltpu.HBM)
    rows = pl.pallas_call(
        kernel,
        out_shape=pltpu.VMEM((5 * BS * 8, 128), F32),
        in_specs=[hbm] * 7,
        out_specs=pl.BlockSpec(memory_space=pltpu.VMEM),
        scratch_shapes=[
            pltpu.VMEM((5 * ROWS, 128), F32),
            pltpu.VMEM((5 * BS * 8, 128), F32),
            pltpu.VMEM((5 * BS * 8, 128), F32),
            pltpu.VMEM((3 * ROWS, 128), F32),
            pltpu.VMEM((STEPS, NB, 16, 128), BF16),
            pltpu.VMEM((NB, 16, 128), BF16),
            pltpu.VMEM((NB, 16, 128), BF16),
            pltpu.VMEM((STEPS, 2, NB, 16, 128), BF16),
            pltpu.VMEM((STEPS, NB + 6, 16, 128), BF16),
            pltpu.VMEM((16, 128), BF16),
            pltpu.VMEM((1, NB), jnp.int32),
            pltpu.VMEM((1, NB), jnp.int32),
            pltpu.VMEM((1, NB), jnp.int32),
            pltpu.VMEM((6, NB), jnp.int32),
            pltpu.VMEM((6, NB), jnp.int32),
            pltpu.VMEM((24, 128), jnp.int32),
            pltpu.VMEM((24, 128), jnp.int32),
            pltpu.SMEM((24, 128), jnp.int32),
            pltpu.SemaphoreType.DMA((5,)),
            pltpu.SemaphoreType.DMA((2,)),
            pltpu.SemaphoreType.DMA(()),
            pltpu.SemaphoreType.DMA((STEPS,)),
            pltpu.SemaphoreType.DMA((STEPS,)),
            pltpu.SemaphoreType.DMA((2 * STEPS,)),
            pltpu.SemaphoreType.DMA((STEPS,)),
            pltpu.SemaphoreType.DMA((STEPS,)),
            pltpu.SemaphoreType.REGULAR,
        ],
        compiler_params=pltpu.CompilerParams(
            collective_id=0, has_side_effects=True, vmem_limit_bytes=60 << 20
        ),
    )(les_owner[None], ac_owner[None], coupling[None], les_nbr.T, ac_nbr.T, state, mean_flow)
    tiles = rows.reshape(5, BS // 8, 8, 8, 128).transpose(0, 1, 3, 2, 4)
    return tiles.reshape(state.shape)


def solution(mesh):
    placed = (P("section", "block"), P("block"), P(), P(), P(), P(), P())
    return jax.shard_map(
        on_device, mesh=mesh, in_specs=placed, out_specs=P("section", "block"), check_vma=False
    )
```

```python
import functools

import jax
import jax.numpy as jnp
from jax import lax
from jax.experimental import pallas as pl
from jax.experimental.pallas import tpu as pltpu
from jax.sharding import PartitionSpec as P

STEPS = 2
NB = 64
BS = 32
PAD = BS + 2
ROWS = PAD * 8
NCELL = 48
MESH = pl.DeviceIdType.MESH
F32 = jnp.float32
BF16 = jnp.bfloat16


def links(t):
    return sum((0, 1, 2, 1)[(t >> shift) & 3] for shift in (0, 2, 4))


ORDER = sorted((42 ^ n for n in range(NB) if n != 42), key=lambda t: -links(t))


def kernel(les_owner, ac_owner, coupling, les_nbr, ac_nbr, state_hbm, mean_hbm, out_ref, q, acc, mean, ul, tile_a, recv_0, recv_1, sort_b, land, pick_ref,
           list_0, list_1, list_2, near_0, near_1, idx_v, tab_v, tab, idx_sem, load_sem, tab_sem, sa, ra, sb, rb, rv, side_sem):
    section = lax.axis_index("section")
    me = lax.axis_index("block")
    les = section == 0
    acoustic = section == 1
    q4 = q.reshape(5, PAD, 8, 128)
    acc4 = acc.reshape(5, BS, 8, 128)
    mean4 = mean.reshape(5, BS, 8, 128)

    barrier = pltpu.get_barrier_semaphore()

    for bits in ORDER:
        pl.semaphore_signal(barrier, inc=1, device_id=(section, me ^ bits), device_id_type=MESH)
    pl.semaphore_signal(barrier, inc=1, device_id=(1 - section, me), device_id_type=MESH)

    recv_a = (recv_0, recv_1)

    def load_copy(c):
        return pltpu.make_async_copy(
            state_hbm.at[0, 0, :, :, pl.ds(128 * c, 128)], q4.at[:, pl.ds(1, BS), c, :], load_sem.at[0]
        )

    def mean_copy(c):
        return pltpu.make_async_copy(
            mean_hbm.at[0, :, :, pl.ds(128 * c, 128)], mean4.at[:, :, c, :], load_sem.at[1]
        )

    zero = jnp.zeros((8, 128), F32)
    for v in range(5):
        q[pl.ds(v * ROWS, 8), :] = zero
        q[pl.ds(v * ROWS + ROWS - 8, 8), :] = zero
    for c in range(8):
        load_copy(c).start()
    lists = (list_0, list_1, list_2, near_0, near_1)
    idx_copies = [
        pltpu.make_async_copy(ref, lists[i], idx_sem.at[i])
        for i, ref in enumerate((les_owner, ac_owner, coupling, les_nbr, ac_nbr))
    ]
    for copy in idx_copies:
        copy.start()

    @pl.when(acoustic)
    def _():
        for c in range(8):
            mean_copy(c).start()

    lane = lax.broadcasted_iota(jnp.int32, (8, 128), 1)
    sub = lax.broadcasted_iota(jnp.int32, (8, 128), 0)
    zpos = lane % BS
    z_low = zpos == 0
    z_high = zpos == BS - 1
    even = lane % 2 == 0

    def up_y(v):
        r = pltpu.roll(v, 96, 1)
        return jnp.where(lane < 96, r, jnp.where(sub < 7, pltpu.roll(r, 7, 0), 0.0))

    def dn_y(v):
        r = pltpu.roll(v, 32, 1)
        return jnp.where(lane >= 32, r, jnp.where(sub > 0, pltpu.roll(r, 1, 0), 0.0))

    def up_z(v):
        return jnp.where(z_high, 0.0, pltpu.roll(v, 127, 1))

    def dn_z(v):
        return jnp.where(z_low, 0.0, pltpu.roll(v, 1, 1))

    lane_t = lax.broadcasted_iota(jnp.int32, (16, 128), 1)
    row_t = lax.broadcasted_iota(jnp.int32, (16, 128), 0)
    by_lane = jnp.where(lane_t % 2 == 1, 1.0, 0.0)
    by_row = jnp.where(row_t < 8, 1.0, 0.0)
    idx_v[...] = jnp.zeros((24, 128), jnp.int32)
    pick_ref[...] = jnp.where(me >= NCELL + 10, by_lane, by_row).astype(BF16)

    for s in range(STEPS):
        tile_a[s, NB - 1] = jnp.zeros((16, 128), BF16)
    loaded = q4.at[:, pl.ds(1, BS)]
    pltpu.make_async_copy(loaded, loaded, load_sem.at[0]).wait()

    def slab(v, x):
        return pl.ds(pl.multiple_of(v * ROWS + 8 * x + 8, 8), 8)

    def aslab(v, x):
        return pl.ds(pl.multiple_of(v * BS * 8 + 8 * x, 8), 8)

    @pl.when(les)
    def _():
        def prim(x, carry):
            inv = 1.0 / q[slab(0, x), :]
            for v in range(1, 4):
                q[slab(v, x), :] = q[slab(v, x), :] * inv
            return carry

        lax.fori_loop(0, BS, prim, 0, unroll=4)

    def make_tables():
        row = lax.broadcasted_iota(jnp.int32, (NB, 128), 0)
        col = lax.broadcasted_iota(jnp.int32, (NB, 128), 1)

        def over_lanes(a):
            for shift in (1, 2, 4, 8, 16, 32, 64):
                a = a + pltpu.roll(a, shift, 1)
            return a

        def over_rows(a):
            total = a[:8]
            for i in range(1, 8):
                total = total + a[8 * i:8 * i + 8]
            for shift in (1, 2, 4):
                total = total + pltpu.roll(total, shift, 0)
            return total

        def wide(a):
            return jnp.concatenate([a] * 8, axis=0)

        def column(i):
            line = jnp.broadcast_to(idx_v[pl.ds(i, 1), :], (NB, 128))
            return over_lanes(jnp.where(row == col, line, 0))

        def look(column_table, index_row):
            return over_rows(jnp.where(row == wide(index_row), column_table, 0))

        les_col, ac_col, link_col = column(0), column(1), column(2)
        own_col = jnp.where(les, les_col, ac_col)
        near_at = jnp.where(les, 8, 16)
        inv_own = over_rows(jnp.where(own_col == col, row, 0))
        inv_ac = over_rows(jnp.where(ac_col == col, row, 0))
        linked = look(link_col, inv_ac)
        coupled = look(les_col, linked)
        inv_les = over_rows(jnp.where(les_col == col, row, 0))
        feed = over_rows(jnp.where(link_col == wide(inv_les), ac_col, 0))
        cells = jnp.where(les, coupled, feed)
        axis_k = jnp.maximum(me - NCELL, 0) // 5
        rows = []
        for side in range(2):
            d = 2 * axis_k + side
            near_col = column(near_at + d)
            first = jnp.where(me < NCELL, cells, look(own_col, look(near_col, inv_own)))
            second = look(own_col, look(near_col, linked))
            rows.append((first, second))
        own_row = idx_v[pl.ds(jnp.where(les, 0, 1), 1), :]
        linked_me = over_rows(jnp.where(ac_col == me, link_col, 0))
        own_near = idx_v[pl.ds(pl.multiple_of(near_at, 8), 8), :]
        in_use = lane < NB
        mine = over_lanes(jnp.where((own_row == me) & in_use, own_near, 0))
        theirs = over_lanes(jnp.where((lane == linked_me) & in_use, idx_v[8:16, :], 0))
        out = jnp.zeros((8, 128), jnp.int32)
        for i, part in enumerate([rows[0][0], rows[1][0], rows[0][1], rows[1][1]]):
            out = jnp.where(sub == i, part, out)
        tab_v[0:8, :] = out
        tab_v[8:16, :] = mine
        tab_v[16:24, :] = theirs
        pltpu.make_async_copy(tab_v, tab, tab_sem).start()

    def pack(s):
        def cells(p, carry):
            for c in range(3):
                start = pl.multiple_of((c + 1) * ROWS + 16 * p + 8, 8)
                tile_a[s, c * 16 + p] = q[pl.ds(start, 16), :].astype(BF16)
            return carry

        lax.fori_loop(0, 16, cells, 0, unroll=4)

        def faces(v, carry):
            tile_a[s, NCELL + v] = jnp.concatenate(
                [q[slab(v, BS - 1), :], q[slab(v, 0), :]], axis=0
            ).astype(BF16)
            base = v * ROWS + 8
            low = high = zero
            for g in range(4):
                group = lane // 32 == g
                a = q[pl.ds(base + 64 * g, 8, stride=8), :]
                b = q[pl.ds(base + 64 * g + 7, 8, stride=8), :]
                low = jnp.where(group, a if g == 0 else pltpu.roll(a, 32 * g, 1), low)
                high = jnp.where(group, b if g == 3 else pltpu.roll(b, 32 * g + 32, 1), high)
            tile_a[s, NCELL + 5 + v] = jnp.concatenate([high, low], axis=0).astype(BF16)
            halves = []
            for half in range(2):
                packed = zero
                for x in range(16):
                    one = q[slab(v, 16 * half + x), :]
                    turned = one if x == 0 else pltpu.roll(one, 2 * x, 1)
                    packed = jnp.where(((lane + 1) % 32) // 2 == x, turned, packed)
                halves.append(packed)
            tile_a[s, NCELL + 10 + v] = jnp.concatenate(halves, axis=0).astype(BF16)
            return carry

        lax.fori_loop(0, 5, faces, 0)

    def others(go):
        for bits in ORDER:
            go(me ^ bits)

    def send_a(s):
        def go(j):
            pltpu.make_async_remote_copy(
                src_ref=tile_a.at[s, j], dst_ref=recv_a[s].at[me], send_sem=sa.at[s], recv_sem=ra.at[s],
                device_id=(section, j), device_id_type=MESH,
            ).start()

        others(go)
        pltpu.make_async_copy(tile_a.at[s, me], recv_a[s].at[me], ra.at[s]).start()

    def put(v, x, value, last):
        if last:
            out_ref[pl.ds(v * BS * 8 + 64 * (x // 8) + x % 8, 8, stride=8), :] = value
        else:
            q[slab(v, x), :] = value

    def les_terms(r, u, v, w, e, axis_k):
        vel = (u, v, w)
        m = (r * u, r * v, r * w)
        p = 0.4 * (e - 0.5 * (m[0] * u + m[1] * v + m[2] * w))
        speed = vel[axis_k]
        flux = [m[axis_k]] + [m[j] * speed + (p if j == axis_k else 0.0) for j in range(3)] + [(e + p) * speed]
        return (r,) + m + (e,), flux

    def les_interior():
        def body(x, carry):
            prev, plus = carry
            f = [q[slab(v, x), :] for v in range(5)]
            r, u, v_, w, e = f
            vel = (u, v_, w)
            m = (r * u, r * v_, r * w)
            p = 0.4 * (e - 0.5 * (m[0] * u + m[1] * v_ + m[2] * w))
            cons = (r,) + m + (e,)
            ep = e + p
            fluxes = []
            for k in range(3):
                sp = 0.1 * vel[k]
                fl = [0.1 * m[k]]
                for j in range(3):
                    t = m[j] * sp
                    if j == k:
                        t = t + 0.1 * p
                    fl.append(t)
                fl.append(ep * sp)
                fluxes.append(fl)
            new, nplus = [], []
            for i in range(5):
                d = 0.01 * cons[i]
                acc[aslab(i, jnp.maximum(x - 1, 0)), :] = prev[i] + (d - fluxes[0][i])
                total = 0.94 * cons[i] + plus[i]
                total = total + (up_y(d - fluxes[1][i]) + dn_y(d + fluxes[1][i]))
                total = total + (up_z(d - fluxes[2][i]) + dn_z(d + fluxes[2][i]))
                new.append(total)
                nplus.append(d + fluxes[0][i])
            return tuple(new), tuple(nplus)

        last, _ = lax.fori_loop(0, BS, body, ((zero,) * 5, (zero,) * 5))
        for i in range(5):
            acc[aslab(i, BS - 1), :] = last[i]

    def ac_interior():
        def body(x, carry):
            here = [q[slab(v, x), :] for v in range(5)]
            dx = [0.5 * (q[slab(v, x + 1), :] - q[slab(v, x - 1), :]) for v in range(5)]
            dy = [0.5 * (up_y(here[v]) - dn_y(here[v])) for v in range(5)]
            dz = [0.5 * (up_z(here[v]) - dn_z(here[v])) for v in range(5)]
            rho, wx, wy, wz, prs = [mean[aslab(v, x), :] for v in range(5)]
            inv = 1.0 / rho
            div = dx[1] + dy[2] + dz[3]
            adv = [wx * dx[v] + wy * dy[v] + wz * dz[v] for v in range(5)]
            extra = [rho * div, dx[4] * inv, dy[4] * inv, dz[4] * inv, (1.4 * prs) * div]
            for v in range(5):
                acc[aslab(v, x), :] = here[v] - 0.3 * (adv[v] + extra[v])
            return carry

        lax.fori_loop(0, BS, body, 0)

    def send_b(s):
        target = jnp.where(me < NCELL, 1 - section, section)
        face_id = me - NCELL
        axis_k = face_id // 5
        comp = face_id % 5 - 1
        tangential = les & (face_id >= 0) & (face_id < 15) & (comp >= 0) & (comp < 3) & (comp != axis_k)
        vel_slot = NB + jnp.maximum(2 * axis_k + comp - jnp.where(comp > axis_k, 1, 0), 0)
        from_low = pick_ref[...] > 0.5

        def join(slot, dest):
            low, high = recv_a[s][tab[2 * slot, dest]], recv_a[s][tab[2 * slot + 1, dest]]
            sort_b[s, slot, dest] = jnp.where(from_low, low, high)

        def send_main(dest):
            join(0, dest)
            pltpu.make_async_remote_copy(
                src_ref=sort_b.at[s, 0, dest], dst_ref=land.at[s, me], send_sem=sb.at[s],
                recv_sem=rb.at[s], device_id=(target, dest), device_id_type=MESH,
            ).start()

        def send_vel(dest):
            join(1, dest)
            pltpu.make_async_remote_copy(
                src_ref=sort_b.at[s, 1, dest], dst_ref=land.at[s, vel_slot], send_sem=sb.at[STEPS + s],
                recv_sem=rv.at[s], device_id=(1, dest), device_id_type=MESH,
            ).start()

        @pl.when((me != NB - 1) & jnp.logical_not(tangential))
        def _():
            others(send_main)

            @pl.when(me < NCELL)
            def _():
                send_main(me)

        @pl.when(tangential)
        def _():
            others(send_vel)
            send_vel(me)
            others(send_main)

        @pl.when((me >= NCELL) & (me != NB - 1))
        def _():
            join(0, me)
            pltpu.make_async_copy(sort_b.at[s, 0, me], land.at[s, me], rb.at[s]).start()

        return tangential

    def tile(ref, *idx):
        return ref[idx].astype(F32)

    def halo_rows(s, axis_k, v):
        got = tile(land, s, NCELL + 5 * axis_k + v)
        own = tile(tile_a, s, NCELL + 5 * axis_k + v)
        low = jnp.where(tab[8 + 2 * axis_k, 0] >= 0, got[:8], own[8:])
        high = jnp.where(tab[9 + 2 * axis_k, 0] >= 0, got[8:], own[:8])
        return low, high

    def turn_z(got, own, f_low, f_high):
        low = jnp.where(f_low >= 0, pltpu.roll(got, 97, 1), own)
        high = jnp.where(f_high >= 0, pltpu.roll(got, 31, 1), own)
        return jnp.where(even, low, high)

    def halo_z(s, v):
        got = tile(land, s, NCELL + 10 + v)
        own = tile(tile_a, s, NCELL + 10 + v)
        return [turn_z(got[8 * h:8 * h + 8], own[8 * h:8 * h + 8], tab[12, 0], tab[13, 0]) for h in range(2)]

    def les_finish(s, last):
        def side_terms(h, axis_k, sign):
            cons, flux = les_terms(*h, axis_k)
            return [0.01 * c + sign * f for c, f in zip(cons, flux)]

        pairs = [halo_rows(s, 0, v) for v in range(5)]
        for side, x, sign in ((0, 0, 0.1), (1, BS - 1, -0.1)):
            terms = side_terms([pr[side] for pr in pairs], 0, sign)
            for v in range(5):
                acc[aslab(v, x), :] = acc[aslab(v, x), :] + terms[v]
        pairs = [halo_rows(s, 1, v) for v in range(5)]
        for side, row, sign in ((0, 0, 0.1), (1, 7, -0.1)):
            terms = side_terms([pr[side] for pr in pairs], 1, sign)
            keep = lane < 32 if side == 0 else lane >= 96
            for v in range(5):
                for g in range(4):
                    amount = (128 - 32 * g if side == 0 else 96 - 32 * g) % 128
                    t = terms[v] if amount == 0 else pltpu.roll(terms[v], amount, 1)
                    where = pl.ds(v * BS * 8 + 64 * g + row, 8, stride=8)
                    acc[where, :] = acc[where, :] + jnp.where(keep, t, 0.0)
        zs = [halo_z(s, v) for v in range(5)]
        sign = jnp.where(even, 0.1, -0.1)
        edge = z_low | z_high
        for half in range(2):
            terms = side_terms([z[half] for z in zs], 2, sign)
            for p in range(8):
                back = [tile(land, s, c * 16 + 8 * half + p) for c in range(3)]
                for o in range(2):
                    x = 16 * half + 2 * p + o
                    new = []
                    for v in range(5):
                        amount = (128 - 2 * (2 * p + o)) % 128
                        t = terms[v] if amount == 0 else pltpu.roll(terms[v], amount, 1)
                        val = acc[aslab(v, x), :] + jnp.where(edge, t, 0.0)
                        if 1 <= v <= 3:
                            val = val + 0.1 * back[v - 1][8 * o:8 * o + 8]
                        new.append(val)
                    if not last:
                        inv = 1.0 / new[0]
                        new = [new[0]] + [new[v] * inv for v in range(1, 4)] + [new[4]]
                    for v in range(5):
                        put(v, x, new[v], last)

    def ac_finish(s, last):
        half_dt = 0.15
        UROWS = PAD * 8

        def uslab(c, x):
            return pl.ds(pl.multiple_of(c * UROWS + 8 * x + 8, 8), 8)

        def unpack(p, carry):
            for c in range(3):
                ul[pl.ds(pl.multiple_of(c * UROWS + 16 * p + 8, 8), 16), :] = tile(land, s, c * 16 + p)
            return carry

        lax.fori_loop(0, 16, unpack, 0, unroll=4)

        pairs = [halo_rows(s, 0, v) for v in range(5)]

        def side_terms(h, m, axis_k, alpha):
            rho, wx, wy, wz, prs = m
            w = (wx, wy, wz)[axis_k]
            terms = [w * h[v] for v in range(5)]
            terms[0] = terms[0] + rho * h[1 + axis_k]
            terms[1 + axis_k] = terms[1 + axis_k] + h[4] / rho
            terms[4] = terms[4] + (1.4 * prs) * h[1 + axis_k]
            return [alpha * t for t in terms]

        for side, x, alpha in ((0, 0, half_dt), (1, BS - 1, -half_dt)):
            m = [mean[aslab(v, x), :] for v in range(5)]
            terms = side_terms([pr[side] for pr in pairs], m, 0, alpha)
            for v in range(5):
                acc[aslab(v, x), :] = acc[aslab(v, x), :] + terms[v]
        pairs_y = [halo_rows(s, 1, v) for v in range(5)]
        zs = [halo_z(s, v) for v in range(5)]

        vel_count = land.at[s, pl.ds(NB, 6)]
        pltpu.make_async_copy(vel_count, vel_count, rv.at[s]).wait()

        vx = [tile(land, s, NB + o) for o in range(2)]
        for o, c in enumerate((1, 2)):
            ul[uslab(c, -1), :] = jnp.where(tab[16, 0] >= 0, vx[o][:8], ul[uslab(c, 0), :])
            ul[uslab(c, BS), :] = jnp.where(tab[17, 0] >= 0, vx[o][8:], ul[uslab(c, BS - 1), :])

        vy = [tile(land, s, NB + 2 + o) for o in range(2)]
        for side, row, alpha in ((0, 0, half_dt), (1, 7, -half_dt)):
            keep = lane < 32 if side == 0 else lane >= 96
            for g in range(4):
                amount = (128 - 32 * g if side == 0 else 96 - 32 * g) % 128

                def turned(t):
                    return t if amount == 0 else pltpu.roll(t, amount, 1)

                def strided(rows, v, lead):
                    return pl.ds(v * rows + lead + 64 * g + row, 8, stride=8)

                m = [mean[strided(BS * 8, v, 0), :] for v in range(5)]
                h = [turned(pr[side]) for pr in pairs_y]
                terms = side_terms(h, m, 1, alpha)
                u = [ul[strided(UROWS, c, 8), :] for c in range(3)]
                hx, hz = [
                    jnp.where(tab[18 + side, 0] >= 0, turned(vy[o][8 * side:8 * side + 8]), u[c])
                    for o, c in enumerate((0, 2))
                ]
                terms[1] = terms[1] + alpha * (u[1] * hx)
                terms[2] = terms[2] - alpha * (hx * u[0] + hz * u[2])
                terms[3] = terms[3] + alpha * (u[1] * hz)
                for v in range(5):
                    where = strided(BS * 8, v, 0)
                    acc[where, :] = acc[where, :] + jnp.where(keep, terms[v], 0.0)

        vz = [tile(land, s, NB + 4 + o) for o in range(2)]
        edge = z_low | z_high
        alpha_z = jnp.where(z_low, half_dt, -half_dt)
        for half in range(2):
            for xx in range(16):
                x = 16 * half + xx
                amount = (128 - 2 * xx) % 128

                def turned(t):
                    return t if amount == 0 else pltpu.roll(t, amount, 1)

                m = [mean[aslab(v, x), :] for v in range(5)]
                h = [turned(zs[v][half]) for v in range(5)]
                terms = side_terms(h, m, 2, alpha_z)
                u = [ul[uslab(c, x), :] for c in range(3)]
                dxv, dxw = [0.5 * (ul[uslab(c, x + 1), :] - ul[uslab(c, x - 1), :]) for c in (1, 2)]
                dyu, dyw = [0.5 * (up_y(u[c]) - dn_y(u[c])) for c in (0, 2)]
                dz = []
                for o, c in enumerate((0, 1)):
                    got = vz[o][8 * half:8 * half + 8]
                    low = pltpu.roll(got, (97 + amount) % 128, 1)
                    high = pltpu.roll(got, (31 + amount) % 128, 1)
                    low = jnp.where(tab[20, 0] >= 0, low, u[c])
                    high = jnp.where(tab[21, 0] >= 0, high, u[c])
                    dz.append(0.5 * (jnp.where(z_high, high, pltpu.roll(u[c], 127, 1))
                                     - jnp.where(z_low, low, pltpu.roll(u[c], 1, 1))))
                dzu, dzv = dz
                ox, oy, oz = dyw - dzv, dzu - dxw, dxv - dyu
                lamb = (oy * u[2] - oz * u[1], oz * u[0] - ox * u[2], ox * u[1] - oy * u[0])
                for v in range(5):
                    val = acc[aslab(v, x), :] + jnp.where(edge, terms[v], 0.0)
                    if 1 <= v <= 3:
                        val = val - 0.3 * lamb[v - 1]
                    put(v, x, val, last)

    pack(0)
    pl.semaphore_wait(barrier, NB)
    pl.semaphore_signal(side_sem, inc=1, device_id=(1 - section, me), device_id_type=MESH)
    send_a(0)

    @pl.when(acoustic)
    def _():
        pltpu.make_async_copy(mean4, mean4, load_sem.at[1]).wait()

    for copy in idx_copies:
        copy.wait()
    for i in range(3):
        idx_v[pl.ds(i, 1), pl.ds(0, NB)] = lists[i][...]
    for i in range(2):
        idx_v[pl.ds(8 + 8 * i, 6), pl.ds(0, NB)] = lists[3 + i][...]
    make_tables()
    for s in range(STEPS):
        if s:
            pack(s)
            send_a(s)

        @pl.when(les)
        def _():
            les_interior()

        @pl.when(acoustic)
        def _():
            ac_interior()

        if s == 0:
            pl.semaphore_wait(side_sem, 1)
            pltpu.make_async_copy(tab_v, tab, tab_sem).wait()
        pltpu.make_async_copy(recv_a[s], recv_a[s], ra.at[s]).wait()
        tangential = send_b(s)
        got = land.at[s, pl.ds(0, NB - 1)]
        pltpu.make_async_copy(got, got, rb.at[s]).wait()

        @pl.when(les)
        def _():
            les_finish(s, s == STEPS - 1)

        @pl.when(acoustic)
        def _():
            ac_finish(s, s == STEPS - 1)

    for s in range(STEPS):
        sent = tile_a.at[s, pl.ds(0, NB - 1)]
        pltpu.make_async_copy(sent, sent, sa.at[s]).wait()

        @pl.when(me != NB - 1)
        def _():
            everyone = sort_b.at[s, 0]
            others = sort_b.at[s, 0, pl.ds(0, NB - 1)]

            @pl.when(me < NCELL)
            def _():
                pltpu.make_async_copy(everyone, everyone, sb.at[s]).wait()

            @pl.when(me >= NCELL)
            def _():
                pltpu.make_async_copy(others, others, sb.at[s]).wait()

        @pl.when(tangential)
        def _():
            extra = sort_b.at[s, 1]
            pltpu.make_async_copy(extra, extra, sb.at[STEPS + s]).wait()


def on_device(state, mean_flow, les_owner, ac_owner, les_nbr, ac_nbr, coupling):
    hbm = pl.BlockSpec(memory_space=pltpu.HBM)
    rows = pl.pallas_call(
        kernel,
        out_shape=pltpu.VMEM((5 * BS * 8, 128), F32),
        in_specs=[hbm] * 7,
        out_specs=pl.BlockSpec(memory_space=pltpu.VMEM),
        scratch_shapes=[
            pltpu.VMEM((5 * ROWS, 128), F32),
            pltpu.VMEM((5 * BS * 8, 128), F32),
            pltpu.VMEM((5 * BS * 8, 128), F32),
            pltpu.VMEM((3 * ROWS, 128), F32),
            pltpu.VMEM((STEPS, NB, 16, 128), BF16),
            pltpu.VMEM((NB, 16, 128), BF16),
            pltpu.VMEM((NB, 16, 128), BF16),
            pltpu.VMEM((STEPS, 2, NB, 16, 128), BF16),
            pltpu.VMEM((STEPS, NB + 6, 16, 128), BF16),
            pltpu.VMEM((16, 128), BF16),
            pltpu.VMEM((1, NB), jnp.int32),
            pltpu.VMEM((1, NB), jnp.int32),
            pltpu.VMEM((1, NB), jnp.int32),
            pltpu.VMEM((6, NB), jnp.int32),
            pltpu.VMEM((6, NB), jnp.int32),
            pltpu.VMEM((24, 128), jnp.int32),
            pltpu.VMEM((24, 128), jnp.int32),
            pltpu.SMEM((24, 128), jnp.int32),
            pltpu.SemaphoreType.DMA((5,)),
            pltpu.SemaphoreType.DMA((2,)),
            pltpu.SemaphoreType.DMA(()),
            pltpu.SemaphoreType.DMA((STEPS,)),
            pltpu.SemaphoreType.DMA((STEPS,)),
            pltpu.SemaphoreType.DMA((2 * STEPS,)),
            pltpu.SemaphoreType.DMA((STEPS,)),
            pltpu.SemaphoreType.DMA((STEPS,)),
            pltpu.SemaphoreType.REGULAR,
        ],
        compiler_params=pltpu.CompilerParams(
            collective_id=0, has_side_effects=True, vmem_limit_bytes=60 << 20
        ),
    )(les_owner[None], ac_owner[None], coupling[None], les_nbr.T, ac_nbr.T, state, mean_flow)
    tiles = rows.reshape(5, BS // 8, 8, 8, 128).transpose(0, 1, 3, 2, 4)
    return tiles.reshape(state.shape)


def solution(mesh):
    placed = (P("section", "block"), P("block"), P(), P(), P(), P(), P())
    return jax.shard_map(
        on_device, mesh=mesh, in_specs=placed, out_specs=P("section", "block"), check_vma=False
    )
```

```python
import functools

import jax
import jax.numpy as jnp
from jax import lax
from jax.experimental import pallas as pl
from jax.experimental.pallas import tpu as pltpu
from jax.sharding import PartitionSpec as P

STEPS = 2
NB = 64
BS = 32
PAD = BS + 2
ROWS = PAD * 8
NCELL = 48
MESH = pl.DeviceIdType.MESH
F32 = jnp.float32
BF16 = jnp.bfloat16


def links(t):
    return sum((0, 1, 2, 1)[(t >> shift) & 3] for shift in (0, 2, 4))


ORDER = sorted((42 ^ n for n in range(NB) if n != 42), key=lambda t: -links(t))


def kernel(les_owner, ac_owner, coupling, les_nbr, ac_nbr, state_hbm, mean_hbm, out_ref, q, acc, mean, ul, tile_a, recv_0, recv_1, sort_b, land, pick_ref,
           list_0, list_1, list_2, near_0, near_1, idx_v, tab_v, tab, idx_sem, load_sem, tab_sem, sa, ra, sb, rb, rv, side_sem):
    section = lax.axis_index("section")
    me = lax.axis_index("block")
    les = section == 0
    acoustic = section == 1
    q4 = q.reshape(5, PAD, 8, 128)
    acc4 = acc.reshape(5, BS, 8, 128)
    mean4 = mean.reshape(5, BS, 8, 128)

    barrier = pltpu.get_barrier_semaphore()

    for bits in ORDER:
        pl.semaphore_signal(barrier, inc=1, device_id=(section, me ^ bits), device_id_type=MESH)
    pl.semaphore_signal(barrier, inc=1, device_id=(1 - section, me), device_id_type=MESH)

    recv_a = (recv_0, recv_1)

    def load_copy(c):
        return pltpu.make_async_copy(
            state_hbm.at[0, 0, :, :, pl.ds(128 * c, 128)], q4.at[:, pl.ds(1, BS), c, :], load_sem.at[0]
        )

    def mean_copy(c):
        return pltpu.make_async_copy(
            mean_hbm.at[0, :, :, pl.ds(128 * c, 128)], mean4.at[:, :, c, :], load_sem.at[1]
        )

    zero = jnp.zeros((8, 128), F32)
    for v in range(5):
        q[pl.ds(v * ROWS, 8), :] = zero
        q[pl.ds(v * ROWS + ROWS - 8, 8), :] = zero
    for c in range(8):
        load_copy(c).start()
    lists = (list_0, list_1, list_2, near_0, near_1)
    idx_copies = [
        pltpu.make_async_copy(ref, lists[i], idx_sem.at[i])
        for i, ref in enumerate((les_owner, ac_owner, coupling, les_nbr, ac_nbr))
    ]
    for copy in idx_copies:
        copy.start()

    @pl.when(acoustic)
    def _():
        for c in range(8):
            mean_copy(c).start()

    lane = lax.broadcasted_iota(jnp.int32, (8, 128), 1)
    sub = lax.broadcasted_iota(jnp.int32, (8, 128), 0)
    zpos = lane % BS
    z_low = zpos == 0
    z_high = zpos == BS - 1
    even = lane % 2 == 0

    def up_y(v):
        r = pltpu.roll(v, 96, 1)
        return jnp.where(lane < 96, r, jnp.where(sub < 7, pltpu.roll(r, 7, 0), 0.0))

    def dn_y(v):
        r = pltpu.roll(v, 32, 1)
        return jnp.where(lane >= 32, r, jnp.where(sub > 0, pltpu.roll(r, 1, 0), 0.0))

    def up_z(v):
        return jnp.where(z_high, 0.0, pltpu.roll(v, 127, 1))

    def dn_z(v):
        return jnp.where(z_low, 0.0, pltpu.roll(v, 1, 1))

    lane_t = lax.broadcasted_iota(jnp.int32, (16, 128), 1)
    row_t = lax.broadcasted_iota(jnp.int32, (16, 128), 0)
    by_lane = jnp.where(lane_t % 2 == 1, 1.0, 0.0)
    by_row = jnp.where(row_t < 8, 1.0, 0.0)
    idx_v[...] = jnp.zeros((24, 128), jnp.int32)
    pick_ref[...] = jnp.where(me >= NCELL + 10, by_lane, by_row).astype(BF16)

    for s in range(STEPS):
        tile_a[s, NB - 1] = jnp.zeros((16, 128), BF16)
    loaded = q4.at[:, pl.ds(1, BS)]
    pltpu.make_async_copy(loaded, loaded, load_sem.at[0]).wait()

    def slab(v, x):
        return pl.ds(pl.multiple_of(v * ROWS + 8 * x + 8, 8), 8)

    def aslab(v, x):
        return pl.ds(pl.multiple_of(v * BS * 8 + 8 * x, 8), 8)

    @pl.when(les)
    def _():
        def prim(x, carry):
            inv = 1.0 / q[slab(0, x), :]
            for v in range(1, 4):
                q[slab(v, x), :] = q[slab(v, x), :] * inv
            return carry

        lax.fori_loop(0, BS, prim, 0, unroll=4)

    def make_tables():
        row = lax.broadcasted_iota(jnp.int32, (NB, 128), 0)
        col = lax.broadcasted_iota(jnp.int32, (NB, 128), 1)

        def over_lanes(a):
            for shift in (1, 2, 4, 8, 16, 32, 64):
                a = a + pltpu.roll(a, shift, 1)
            return a

        def over_rows(a):
            total = a[:8]
            for i in range(1, 8):
                total = total + a[8 * i:8 * i + 8]
            for shift in (1, 2, 4):
                total = total + pltpu.roll(total, shift, 0)
            return total

        def wide(a):
            return jnp.concatenate([a] * 8, axis=0)

        def column(i):
            line = jnp.broadcast_to(idx_v[pl.ds(i, 1), :], (NB, 128))
            return over_lanes(jnp.where(row == col, line, 0))

        def look(column_table, index_row):
            return over_rows(jnp.where(row == wide(index_row), column_table, 0))

        les_col, ac_col, link_col = column(0), column(1), column(2)
        own_col = jnp.where(les, les_col, ac_col)
        near_at = jnp.where(les, 8, 16)
        inv_own = over_rows(jnp.where(own_col == col, row, 0))
        inv_ac = over_rows(jnp.where(ac_col == col, row, 0))
        linked = look(link_col, inv_ac)
        coupled = look(les_col, linked)
        inv_les = over_rows(jnp.where(les_col == col, row, 0))
        feed = over_rows(jnp.where(link_col == wide(inv_les), ac_col, 0))
        cells = jnp.where(les, coupled, feed)
        axis_k = jnp.maximum(me - NCELL, 0) // 5
        rows = []
        for side in range(2):
            d = 2 * axis_k + side
            near_col = column(near_at + d)
            first = jnp.where(me < NCELL, cells, look(own_col, look(near_col, inv_own)))
            second = look(own_col, look(near_col, linked))
            rows.append((first, second))
        own_row = idx_v[pl.ds(jnp.where(les, 0, 1), 1), :]
        linked_me = over_rows(jnp.where(ac_col == me, link_col, 0))
        own_near = idx_v[pl.ds(pl.multiple_of(near_at, 8), 8), :]
        in_use = lane < NB
        mine = over_lanes(jnp.where((own_row == me) & in_use, own_near, 0))
        theirs = over_lanes(jnp.where((lane == linked_me) & in_use, idx_v[8:16, :], 0))
        out = jnp.zeros((8, 128), jnp.int32)
        for i, part in enumerate([rows[0][0], rows[1][0], rows[0][1], rows[1][1]]):
            out = jnp.where(sub == i, part, out)
        tab_v[0:8, :] = out
        tab_v[8:16, :] = mine
        tab_v[16:24, :] = theirs
        pltpu.make_async_copy(tab_v, tab, tab_sem).start()

    def pack(s):
        def cells(p, carry):
            for c in range(3):
                start = pl.multiple_of((c + 1) * ROWS + 16 * p + 8, 8)
                tile_a[s, c * 16 + p] = q[pl.ds(start, 16), :].astype(BF16)
            return carry

        lax.fori_loop(0, 16, cells, 0, unroll=16)

        def faces(v, carry):
            tile_a[s, NCELL + v] = jnp.concatenate(
                [q[slab(v, BS - 1), :], q[slab(v, 0), :]], axis=0
            ).astype(BF16)
            base = v * ROWS + 8
            low = high = zero
            for g in range(4):
                group = lane // 32 == g
                a = q[pl.ds(base + 64 * g, 8, stride=8), :]
                b = q[pl.ds(base + 64 * g + 7, 8, stride=8), :]
                low = jnp.where(group, a if g == 0 else pltpu.roll(a, 32 * g, 1), low)
                high = jnp.where(group, b if g == 3 else pltpu.roll(b, 32 * g + 32, 1), high)
            tile_a[s, NCELL + 5 + v] = jnp.concatenate([high, low], axis=0).astype(BF16)
            halves = []
            for half in range(2):
                packed = zero
                for x in range(16):
                    one = q[slab(v, 16 * half + x), :]
                    turned = one if x == 0 else pltpu.roll(one, 2 * x, 1)
                    packed = jnp.where(((lane + 1) % 32) // 2 == x, turned, packed)
                halves.append(packed)
            tile_a[s, NCELL + 10 + v] = jnp.concatenate(halves, axis=0).astype(BF16)
            return carry

        lax.fori_loop(0, 5, faces, 0, unroll=5)

    def others(go):
        for bits in ORDER:
            go(me ^ bits)

    def send_a(s):
        def go(j):
            pltpu.make_async_remote_copy(
                src_ref=tile_a.at[s, j], dst_ref=recv_a[s].at[me], send_sem=sa.at[s], recv_sem=ra.at[s],
                device_id=(section, j), device_id_type=MESH,
            ).start()

        others(go)
        pltpu.make_async_copy(tile_a.at[s, me], recv_a[s].at[me], ra.at[s]).start()

    def put(v, x, value, last):
        if last:
            out_ref[pl.ds(v * BS * 8 + 64 * (x // 8) + x % 8, 8, stride=8), :] = value
        else:
            q[slab(v, x), :] = value

    def les_terms(r, u, v, w, e, axis_k):
        vel = (u, v, w)
        m = (r * u, r * v, r * w)
        p = 0.4 * (e - 0.5 * (m[0] * u + m[1] * v + m[2] * w))
        speed = vel[axis_k]
        flux = [m[axis_k]] + [m[j] * speed + (p if j == axis_k else 0.0) for j in range(3)] + [(e + p) * speed]
        return (r,) + m + (e,), flux

    def les_interior():
        def body(x, carry):
            prev, plus = carry
            f = [q[slab(v, x), :] for v in range(5)]
            r, u, v_, w, e = f
            vel = (u, v_, w)
            m = (r * u, r * v_, r * w)
            p = 0.4 * (e - 0.5 * (m[0] * u + m[1] * v_ + m[2] * w))
            cons = (r,) + m + (e,)
            ep = e + p
            fluxes = []
            for k in range(3):
                sp = 0.1 * vel[k]
                fl = [0.1 * m[k]]
                for j in range(3):
                    t = m[j] * sp
                    if j == k:
                        t = t + 0.1 * p
                    fl.append(t)
                fl.append(ep * sp)
                fluxes.append(fl)
            new, nplus = [], []
            for i in range(5):
                d = 0.01 * cons[i]
                acc[aslab(i, jnp.maximum(x - 1, 0)), :] = prev[i] + (d - fluxes[0][i])
                total = 0.94 * cons[i] + plus[i]
                total = total + (up_y(d - fluxes[1][i]) + dn_y(d + fluxes[1][i]))
                total = total + (up_z(d - fluxes[2][i]) + dn_z(d + fluxes[2][i]))
                new.append(total)
                nplus.append(d + fluxes[0][i])
            return tuple(new), tuple(nplus)

        last, _ = lax.fori_loop(0, BS, body, ((zero,) * 5, (zero,) * 5))
        for i in range(5):
            acc[aslab(i, BS - 1), :] = last[i]

    def ac_interior():
        def body(x, carry):
            here = [q[slab(v, x), :] for v in range(5)]
            dx = [0.5 * (q[slab(v, x + 1), :] - q[slab(v, x - 1), :]) for v in range(5)]
            dy = [0.5 * (up_y(here[v]) - dn_y(here[v])) for v in range(5)]
            dz = [0.5 * (up_z(here[v]) - dn_z(here[v])) for v in range(5)]
            rho, wx, wy, wz, prs = [mean[aslab(v, x), :] for v in range(5)]
            inv = 1.0 / rho
            div = dx[1] + dy[2] + dz[3]
            adv = [wx * dx[v] + wy * dy[v] + wz * dz[v] for v in range(5)]
            extra = [rho * div, dx[4] * inv, dy[4] * inv, dz[4] * inv, (1.4 * prs) * div]
            for v in range(5):
                acc[aslab(v, x), :] = here[v] - 0.3 * (adv[v] + extra[v])
            return carry

        lax.fori_loop(0, BS, body, 0)

    def send_b(s):
        target = jnp.where(me < NCELL, 1 - section, section)
        face_id = me - NCELL
        axis_k = face_id // 5
        comp = face_id % 5 - 1
        tangential = les & (face_id >= 0) & (face_id < 15) & (comp >= 0) & (comp < 3) & (comp != axis_k)
        vel_slot = NB + jnp.maximum(2 * axis_k + comp - jnp.where(comp > axis_k, 1, 0), 0)
        from_low = pick_ref[...] > 0.5

        def join(slot, dest):
            low, high = recv_a[s][tab[2 * slot, dest]], recv_a[s][tab[2 * slot + 1, dest]]
            sort_b[s, slot, dest] = jnp.where(from_low, low, high)

        def send_main(dest):
            join(0, dest)
            pltpu.make_async_remote_copy(
                src_ref=sort_b.at[s, 0, dest], dst_ref=land.at[s, me], send_sem=sb.at[s],
                recv_sem=rb.at[s], device_id=(target, dest), device_id_type=MESH,
            ).start()

        def send_vel(dest):
            join(1, dest)
            pltpu.make_async_remote_copy(
                src_ref=sort_b.at[s, 1, dest], dst_ref=land.at[s, vel_slot], send_sem=sb.at[STEPS + s],
                recv_sem=rv.at[s], device_id=(1, dest), device_id_type=MESH,
            ).start()

        @pl.when((me != NB - 1) & jnp.logical_not(tangential))
        def _():
            others(send_main)

            @pl.when(me < NCELL)
            def _():
                send_main(me)

        @pl.when(tangential)
        def _():
            for part in (ORDER[:22], ORDER[22:]):
                for send in (send_vel, send_main):
                    for bits in part:
                        send(me ^ bits)
            send_vel(me)

        @pl.when((me >= NCELL) & (me != NB - 1))
        def _():
            join(0, me)
            pltpu.make_async_copy(sort_b.at[s, 0, me], land.at[s, me], rb.at[s]).start()

        return tangential

    def tile(ref, *idx):
        return ref[idx].astype(F32)

    def halo_rows(s, axis_k, v):
        got = tile(land, s, NCELL + 5 * axis_k + v)
        own = tile(tile_a, s, NCELL + 5 * axis_k + v)
        low = jnp.where(tab[8 + 2 * axis_k, 0] >= 0, got[:8], own[8:])
        high = jnp.where(tab[9 + 2 * axis_k, 0] >= 0, got[8:], own[:8])
        return low, high

    def turn_z(got, own, f_low, f_high):
        low = jnp.where(f_low >= 0, pltpu.roll(got, 97, 1), own)
        high = jnp.where(f_high >= 0, pltpu.roll(got, 31, 1), own)
        return jnp.where(even, low, high)

    def halo_z(s, v):
        got = tile(land, s, NCELL + 10 + v)
        own = tile(tile_a, s, NCELL + 10 + v)
        return [turn_z(got[8 * h:8 * h + 8], own[8 * h:8 * h + 8], tab[12, 0], tab[13, 0]) for h in range(2)]

    def les_finish(s, last):
        def side_terms(h, axis_k, sign):
            cons, flux = les_terms(*h, axis_k)
            return [0.01 * c + sign * f for c, f in zip(cons, flux)]

        pairs = [halo_rows(s, 0, v) for v in range(5)]
        for side, x, sign in ((0, 0, 0.1), (1, BS - 1, -0.1)):
            terms = side_terms([pr[side] for pr in pairs], 0, sign)
            for v in range(5):
                acc[aslab(v, x), :] = acc[aslab(v, x), :] + terms[v]
        pairs = [halo_rows(s, 1, v) for v in range(5)]
        for side, row, sign in ((0, 0, 0.1), (1, 7, -0.1)):
            terms = side_terms([pr[side] for pr in pairs], 1, sign)
            keep = lane < 32 if side == 0 else lane >= 96
            for v in range(5):
                for g in range(4):
                    amount = (128 - 32 * g if side == 0 else 96 - 32 * g) % 128
                    t = terms[v] if amount == 0 else pltpu.roll(terms[v], amount, 1)
                    where = pl.ds(v * BS * 8 + 64 * g + row, 8, stride=8)
                    acc[where, :] = acc[where, :] + jnp.where(keep, t, 0.0)
        zs = [halo_z(s, v) for v in range(5)]
        sign = jnp.where(even, 0.1, -0.1)
        edge = z_low | z_high
        for half in range(2):
            terms = side_terms([z[half] for z in zs], 2, sign)
            for p in range(8):
                back = [tile(land, s, c * 16 + 8 * half + p) for c in range(3)]
                for o in range(2):
                    x = 16 * half + 2 * p + o
                    new = []
                    for v in range(5):
                        amount = (128 - 2 * (2 * p + o)) % 128
                        t = terms[v] if amount == 0 else pltpu.roll(terms[v], amount, 1)
                        val = acc[aslab(v, x), :] + jnp.where(edge, t, 0.0)
                        if 1 <= v <= 3:
                            val = val + 0.1 * back[v - 1][8 * o:8 * o + 8]
                        new.append(val)
                    if not last:
                        inv = 1.0 / new[0]
                        new = [new[0]] + [new[v] * inv for v in range(1, 4)] + [new[4]]
                    for v in range(5):
                        put(v, x, new[v], last)

    def ac_finish(s, last):
        half_dt = 0.15
        UROWS = PAD * 8

        def uslab(c, x):
            return pl.ds(pl.multiple_of(c * UROWS + 8 * x + 8, 8), 8)

        def unpack(p, carry):
            for c in range(3):
                ul[pl.ds(pl.multiple_of(c * UROWS + 16 * p + 8, 8), 16), :] = tile(land, s, c * 16 + p)
            return carry

        lax.fori_loop(0, 16, unpack, 0, unroll=16)

        pairs = [halo_rows(s, 0, v) for v in range(5)]

        def side_terms(h, m, axis_k, alpha):
            rho, wx, wy, wz, prs = m
            w = (wx, wy, wz)[axis_k]
            terms = [w * h[v] for v in range(5)]
            terms[0] = terms[0] + rho * h[1 + axis_k]
            terms[1 + axis_k] = terms[1 + axis_k] + h[4] / rho
            terms[4] = terms[4] + (1.4 * prs) * h[1 + axis_k]
            return [alpha * t for t in terms]

        for side, x, alpha in ((0, 0, half_dt), (1, BS - 1, -half_dt)):
            m = [mean[aslab(v, x), :] for v in range(5)]
            terms = side_terms([pr[side] for pr in pairs], m, 0, alpha)
            for v in range(5):
                acc[aslab(v, x), :] = acc[aslab(v, x), :] + terms[v]
        pairs_y = [halo_rows(s, 1, v) for v in range(5)]
        zs = [halo_z(s, v) for v in range(5)]

        vel_count = land.at[s, pl.ds(NB, 6)]
        pltpu.make_async_copy(vel_count, vel_count, rv.at[s]).wait()

        vx = [tile(land, s, NB + o) for o in range(2)]
        for o, c in enumerate((1, 2)):
            ul[uslab(c, -1), :] = jnp.where(tab[16, 0] >= 0, vx[o][:8], ul[uslab(c, 0), :])
            ul[uslab(c, BS), :] = jnp.where(tab[17, 0] >= 0, vx[o][8:], ul[uslab(c, BS - 1), :])

        vy = [tile(land, s, NB + 2 + o) for o in range(2)]
        for side, row, alpha in ((0, 0, half_dt), (1, 7, -half_dt)):
            keep = lane < 32 if side == 0 else lane >= 96
            for g in range(4):
                amount = (128 - 32 * g if side == 0 else 96 - 32 * g) % 128

                def turned(t):
                    return t if amount == 0 else pltpu.roll(t, amount, 1)

                def strided(rows, v, lead):
                    return pl.ds(v * rows + lead + 64 * g + row, 8, stride=8)

                m = [mean[strided(BS * 8, v, 0), :] for v in range(5)]
                h = [turned(pr[side]) for pr in pairs_y]
                terms = side_terms(h, m, 1, alpha)
                u = [ul[strided(UROWS, c, 8), :] for c in range(3)]
                hx, hz = [
                    jnp.where(tab[18 + side, 0] >= 0, turned(vy[o][8 * side:8 * side + 8]), u[c])
                    for o, c in enumerate((0, 2))
                ]
                terms[1] = terms[1] + alpha * (u[1] * hx)
                terms[2] = terms[2] - alpha * (hx * u[0] + hz * u[2])
                terms[3] = terms[3] + alpha * (u[1] * hz)
                for v in range(5):
                    where = strided(BS * 8, v, 0)
                    acc[where, :] = acc[where, :] + jnp.where(keep, terms[v], 0.0)

        vz = []
        for o in range(2):
            got = tile(land, s, NB + 4 + o)
            vz.append([
                jnp.where(even, pltpu.roll(got[8 * h:8 * h + 8], 97, 1), pltpu.roll(got[8 * h:8 * h + 8], 31, 1))
                for h in range(2)
            ])
        edge = z_low | z_high
        alpha_z = jnp.where(z_low, half_dt, -half_dt)
        for half in range(2):
            for xx in range(16):
                x = 16 * half + xx
                amount = (128 - 2 * xx) % 128

                def turned(t):
                    return t if amount == 0 else pltpu.roll(t, amount, 1)

                m = [mean[aslab(v, x), :] for v in range(5)]
                h = [turned(zs[v][half]) for v in range(5)]
                terms = side_terms(h, m, 2, alpha_z)
                u = [ul[uslab(c, x), :] for c in range(3)]
                dxv, dxw = [0.5 * (ul[uslab(c, x + 1), :] - ul[uslab(c, x - 1), :]) for c in (1, 2)]
                dyu, dyw = [0.5 * (up_y(u[c]) - dn_y(u[c])) for c in (0, 2)]
                dz = []
                for o, c in enumerate((0, 1)):
                    got = turned(vz[o][half])
                    low = jnp.where(tab[20, 0] >= 0, got, u[c])
                    high = jnp.where(tab[21, 0] >= 0, got, u[c])
                    dz.append(0.5 * (jnp.where(z_high, high, pltpu.roll(u[c], 127, 1))
                                     - jnp.where(z_low, low, pltpu.roll(u[c], 1, 1))))
                dzu, dzv = dz
                ox, oy, oz = dyw - dzv, dzu - dxw, dxv - dyu
                lamb = (oy * u[2] - oz * u[1], oz * u[0] - ox * u[2], ox * u[1] - oy * u[0])
                for v in range(5):
                    val = acc[aslab(v, x), :] + jnp.where(edge, terms[v], 0.0)
                    if 1 <= v <= 3:
                        val = val - 0.3 * lamb[v - 1]
                    put(v, x, val, last)

    pack(0)
    pl.semaphore_wait(barrier, NB)
    pl.semaphore_signal(side_sem, inc=1, device_id=(1 - section, me), device_id_type=MESH)
    send_a(0)

    @pl.when(acoustic)
    def _():
        pltpu.make_async_copy(mean4, mean4, load_sem.at[1]).wait()

    for copy in idx_copies:
        copy.wait()
    for i in range(3):
        idx_v[pl.ds(i, 1), pl.ds(0, NB)] = lists[i][...]
    for i in range(2):
        idx_v[pl.ds(8 + 8 * i, 6), pl.ds(0, NB)] = lists[3 + i][...]
    make_tables()
    for s in range(STEPS):
        if s:
            pack(s)
            send_a(s)

        @pl.when(les)
        def _():
            les_interior()

        @pl.when(acoustic)
        def _():
            ac_interior()

        if s == 0:
            pl.semaphore_wait(side_sem, 1)
            pltpu.make_async_copy(tab_v, tab, tab_sem).wait()
        pltpu.make_async_copy(recv_a[s], recv_a[s], ra.at[s]).wait()
        tangential = send_b(s)
        got = land.at[s, pl.ds(0, NB - 1)]
        pltpu.make_async_copy(got, got, rb.at[s]).wait()

        @pl.when(les)
        def _():
            les_finish(s, s == STEPS - 1)

        @pl.when(acoustic)
        def _():
            ac_finish(s, s == STEPS - 1)

    for s in range(STEPS):
        sent = tile_a.at[s, pl.ds(0, NB - 1)]
        pltpu.make_async_copy(sent, sent, sa.at[s]).wait()

        @pl.when(me != NB - 1)
        def _():
            everyone = sort_b.at[s, 0]
            others = sort_b.at[s, 0, pl.ds(0, NB - 1)]

            @pl.when(me < NCELL)
            def _():
                pltpu.make_async_copy(everyone, everyone, sb.at[s]).wait()

            @pl.when(me >= NCELL)
            def _():
                pltpu.make_async_copy(others, others, sb.at[s]).wait()

        @pl.when(tangential)
        def _():
            extra = sort_b.at[s, 1]
            pltpu.make_async_copy(extra, extra, sb.at[STEPS + s]).wait()


def on_device(state, mean_flow, les_owner, ac_owner, les_nbr, ac_nbr, coupling):
    hbm = pl.BlockSpec(memory_space=pltpu.HBM)
    rows = pl.pallas_call(
        kernel,
        out_shape=pltpu.VMEM((5 * BS * 8, 128), F32),
        in_specs=[hbm] * 7,
        out_specs=pl.BlockSpec(memory_space=pltpu.VMEM),
        scratch_shapes=[
            pltpu.VMEM((5 * ROWS, 128), F32),
            pltpu.VMEM((5 * BS * 8, 128), F32),
            pltpu.VMEM((5 * BS * 8, 128), F32),
            pltpu.VMEM((3 * ROWS, 128), F32),
            pltpu.VMEM((STEPS, NB, 16, 128), BF16),
            pltpu.VMEM((NB, 16, 128), BF16),
            pltpu.VMEM((NB, 16, 128), BF16),
            pltpu.VMEM((STEPS, 2, NB, 16, 128), BF16),
            pltpu.VMEM((STEPS, NB + 6, 16, 128), BF16),
            pltpu.VMEM((16, 128), BF16),
            pltpu.VMEM((1, NB), jnp.int32),
            pltpu.VMEM((1, NB), jnp.int32),
            pltpu.VMEM((1, NB), jnp.int32),
            pltpu.VMEM((6, NB), jnp.int32),
            pltpu.VMEM((6, NB), jnp.int32),
            pltpu.VMEM((24, 128), jnp.int32),
            pltpu.VMEM((24, 128), jnp.int32),
            pltpu.SMEM((24, 128), jnp.int32),
            pltpu.SemaphoreType.DMA((5,)),
            pltpu.SemaphoreType.DMA((2,)),
            pltpu.SemaphoreType.DMA(()),
            pltpu.SemaphoreType.DMA((STEPS,)),
            pltpu.SemaphoreType.DMA((STEPS,)),
            pltpu.SemaphoreType.DMA((2 * STEPS,)),
            pltpu.SemaphoreType.DMA((STEPS,)),
            pltpu.SemaphoreType.DMA((STEPS,)),
            pltpu.SemaphoreType.REGULAR,
        ],
        compiler_params=pltpu.CompilerParams(
            collective_id=0, has_side_effects=True, vmem_limit_bytes=60 << 20
        ),
    )(les_owner[None], ac_owner[None], coupling[None], les_nbr.T, ac_nbr.T, state, mean_flow)
    tiles = rows.reshape(5, BS // 8, 8, 8, 128).transpose(0, 1, 3, 2, 4)
    return tiles.reshape(state.shape)


def solution(mesh):
    placed = (P("section", "block"), P("block"), P(), P(), P(), P(), P())
    return jax.shard_map(
        on_device, mesh=mesh, in_specs=placed, out_specs=P("section", "block"), check_vma=False
    )
```
